256 devices in a mesh: row: 8 (over x_lo, y), col: 32 (over z, x_hi, core).
Axes of the slice: x: 4 (x_hi: 2, x_lo: 2; x = x_hi * 2 + x_lo), y: 4, z: 8, core: 2. Of those that a mesh axis runs over, the one named last changes fastest.
Arguments:
- weight: bfloat16 [4096, 8192], P('row', 'col'), may hold values from -6 to 6
- grad: bfloat16 [4096, 8192], P('row', 'col'), may hold values from -6 to 6
- moment_first: float32 [4096, 8192], P('row', 'col'), may hold values from -2 to 2
- moment_second: float32 [4096, 8192], P('row', 'col'), may hold values from 0.05 to 5
- basis_left: bfloat16 [4096, 4096], P('col', 'row'), may hold values from -0.13 to 1.13
- basis_right: bfloat16 [8192, 8192], P('col', 'row'), may hold values from -0.13 to 1.13
Outputs:
- new_weight: bfloat16 [4096, 8192], P('row', 'col')
- update: bfloat16 [4096, 8192], P('row', 'col')
- first_new: float32 [4096, 8192], P('row', 'col')
- second_new: float32 [4096, 8192], P('row', 'col')
The draws below stay inside these ranges and needn't reach their ends.
All inputs are finite; a program needn't handle non-finite values.
Results may differ from the reference program's by a relative error of at most 0.018.
Values may be sent and summed in bfloat16 or wider, within the bound.
A program may use at most 128 MiB of HBM per device.

```python
import math
import jax
import jax.numpy as jnp
from jax import lax

M = 4096
N = 8192
N_ROW = 8
N_COL = 32


def make_basis(key, order):
    noise = jax.random.truncated_normal(key, -4.0, 4.0, (order, order), jnp.float32)
    return jnp.eye(order, dtype=jnp.float32) + noise * (0.5 / order ** 0.5)


def draw_basis_left(key, part):
    key = jax.random.fold_in(key, 1)
    return make_basis(key, M).astype(jnp.bfloat16)


def draw_basis_right(key, part):
    key = jax.random.fold_in(key, 2)
    return make_basis(key, N).astype(jnp.bfloat16)


def block_levels(own_key, dims, cuts, smallest, high):
    level, own = 1.0, jax.random.fold_in(own_key, 6)
    for dim, shards_of in cuts:
        heights = jnp.exp(jax.random.uniform(jax.random.fold_in(own, dim), (shards_of,), jnp.float32, smallest / len(cuts), high / len(cuts)))
        level = level * jnp.repeat(heights, dims[dim] // shards_of).reshape([-1 if axis == dim else 1 for axis in range(len(dims))])
    return level


def normal_values(rng, shape, deviation, most, split=(), held_as=jnp.bfloat16):
    array = jax.random.normal(rng, shape, jnp.float32) * deviation
    if len(split) > 0:
        array = block_levels(rng, shape, split, -0.22, 0.18) * array
    return jnp.clip(array, min=-most, max=most).astype(held_as)


def setup_inputs(seed: int = 0) -> dict:
    splits = jax.random.split(jax.random.key(seed), 7)
    weight = normal_values(splits[0], (M, N), 1.0, 6.0, ((0, 8), (1, 32)))
    grad = normal_values(splits[1], (M, N), 1.0, 6.0, ((0, 8), (1, 32)))
    moment_first = normal_values(splits[2], (M, N), 0.3, 2.0, ((0, 8), (1, 32)), jnp.float32)
    moment_second = jnp.clip(jnp.exp(math.log(5.0) - 4.6051702 * jax.random.uniform(splits[3], (M, N), jnp.float32) ** block_levels(splits[3], (M, N), ((0, 8), (1, 32)), -0.2, 0.2)), 0.05, 5.0)
    basis_left = draw_basis_left(jax.random.fold_in(splits[6], 71), 0)
    basis_right = draw_basis_right(jax.random.fold_in(splits[6], 71), 0)
    return {"weight": weight, "grad": grad, "moment_first": moment_first, "moment_second": moment_second, "basis_left": basis_left, "basis_right": basis_right}


beta_first = 0.9
beta_second = 0.95
correct_first = 1.0 - 0.9 ** 10
correct_second = 1.0 - 0.95 ** 10
epsilon = 1e-08
learn_rate = 0.001
decay_rate = 0.1

def reference(weight, grad, moment_first, moment_second, basis_left, basis_right):
    width = N // N_COL

    def add_block(total, index):
        start = (index * width).astype(jnp.int32)
        grad_cols = lax.dynamic_slice_in_dim(grad, start, width, 1)
        basis_rows = lax.dynamic_slice_in_dim(basis_right, start, width, 0)
        term = jnp.dot(grad_cols, basis_rows, preferred_element_type=jnp.float32)
        rounded = lax.optimization_barrier(term.astype(jnp.bfloat16))
        return (total + rounded.astype(jnp.float32), None)
    right_sum, _ = lax.scan(add_block, jnp.zeros((M, N), jnp.float32), jnp.arange(N_COL, dtype=jnp.int32))
    half_rotated = right_sum.astype(jnp.bfloat16)
    rotated = jnp.dot(basis_left.T, half_rotated, preferred_element_type=jnp.float32)
    first_new = beta_first * moment_first + (1.0 - beta_first) * rotated
    second_new = beta_second * moment_second + (1.0 - beta_second) * rotated * rotated
    step_rotated = (first_new / correct_first / (jnp.sqrt(second_new / correct_second) + epsilon)).astype(jnp.bfloat16)
    height = M // N_ROW

    def add_left(total, index):
        start = (index * height).astype(jnp.int32)
        basis_cols = lax.dynamic_slice_in_dim(basis_left, start, height, 1)
        step_rows = lax.dynamic_slice_in_dim(step_rotated, start, height, 0)
        term = jnp.dot(basis_cols, step_rows, preferred_element_type=jnp.float32)
        rounded = lax.optimization_barrier(term.astype(jnp.bfloat16))
        return (total + rounded.astype(jnp.float32), None)
    left_back, _ = lax.scan(add_left, jnp.zeros((M, N), jnp.float32), jnp.arange(N_ROW, dtype=jnp.int32))
    back_half = left_back.astype(jnp.bfloat16)
    direction = jnp.dot(back_half, basis_right.T, preferred_element_type=jnp.float32)
    update = direction.astype(jnp.bfloat16)
    weight_wide = weight.astype(jnp.float32)
    new_weight = (weight_wide - learn_rate * (direction + decay_rate * weight_wide)).astype(jnp.bfloat16)
    return (new_weight, update, first_new, second_new)
```

```python
import jax
import jax.numpy as jnp
from jax import lax
from jax.experimental import pallas as pl
from jax.experimental.pallas import tpu as pltpu
from jax.sharding import PartitionSpec as P

beta_first = 0.9
beta_second = 0.95
correct_first = 1.0 - 0.9**10
correct_second = 1.0 - 0.95**10
epsilon = 1e-08
learn_rate = 0.001
decay_rate = 0.1

ROWS = 512
COLS = 256
HALF = 128
N_MSG = 160

f32 = jnp.float32
bf16 = jnp.bfloat16


def kernel(
    weight, grad, moment_first, moment_second, ql, qr,
    new_weight, update, first_new, second_new,
    qr_all, g_all, ql_all, t_all, p_send, p_recv, b_part, b_send, b_recv, b_all,
    d_acc, d_send, d_recv, send_sem, recv_sem,
):
    row, col = lax.axis_index("row"), lax.axis_index("col")
    xl, y = lax.div(row, 4), lax.rem(row, 4)
    z, u = lax.div(col, 4), lax.rem(col, 4)
    xh, k = lax.div(u, 2), lax.rem(u, 2)

    def ring(value, shift, size):
        return lax.rem(value + (shift + size), size)

    u_core = xh * 2 + (1 - k)
    u_far = (1 - xh) * 2 + k
    u_cross = (1 - xh) * 2 + (1 - k)
    z_at = lambda s: ring(z, s, 8)
    row_at = lambda side, s: (xl if side == 0 else 1 - xl) * 4 + ring(y, s, 4)
    to_core = (row, z * 4 + u_core)
    to_far = (row, z * 4 + u_far)
    to_cross = (row, z * 4 + u_cross)
    to_z = {s: (row, z_at(s) * 4 + u) for s in (1, -1)}
    to_y = {s: (row_at(0, s), col) for s in (1, -1)}
    to_x = (row_at(1, 0), col)

    started = []

    def send(src, dst, to):
        n = len(started)
        copy = pltpu.make_async_remote_copy(
            src_ref=src, dst_ref=dst, send_sem=send_sem.at[n], recv_sem=recv_sem.at[n],
            device_id=to, device_id_type=pl.DeviceIdType.MESH,
        )
        copy.start()
        started.append(copy)
        return copy

    def lanes(index, width):
        return pl.ds(pl.multiple_of(index * width, width), width)

    barrier = pltpu.get_barrier_semaphore()
    partners = (to_core, to_far, to_cross, to_z[1], to_z[-1], to_y[1], to_y[-1], to_x)
    for partner in partners:
        pl.semaphore_signal(
            barrier, inc=1, device_id=partner, device_id_type=pl.DeviceIdType.MESH
        )
    pl.semaphore_wait(barrier, len(partners))

    near_in = send(qr.at[:, lanes(u_core, COLS)], qr_all.at[row, u], to_core)
    far_in = send(qr.at[:, lanes(u_far, COLS)], qr_all.at[row, u], to_far)
    cross_in = send(qr.at[:, lanes(u_cross, COLS)], qr_all.at[row, u], to_cross)
    g_core = send(grad, g_all.at[:, lanes(u, COLS)], to_core)
    ql_core = send(ql, ql_all.at[z, xh, k], to_core)
    qr_all[row, u] = qr[:, lanes(u, COLS)]
    g_all[:, lanes(u, COLS)] = grad[...]
    ql_all[z, xh, k] = ql[...]

    def piece(owner, pair):
        return qr_all.at[owner, pl.ds(pair * 2, 2)]

    def part(owner, pair, n):
        return qr_all.at[owner, pair * 2 + n]

    def spread(ref, owner):
        view = ref(owner)
        return [send(view, view, to_x), send(view, view, to_y[1]), send(view, view, to_y[-1])]

    near_in.wait_recv()
    near = spread(lambda o: piece(o, xh), row)
    far_in.wait_recv()
    cross_in.wait_recv()
    far = spread(lambda o: piece(o, 1 - xh), row)
    g_far = send(grad, g_all.at[:, lanes(u, COLS)], to_far)
    ql_far = send(ql, ql_all.at[z, xh, k], to_far)

    later = []

    def spread_second(first, pair):
        other = row_at(1, 0)
        first[0].wait_recv()
        for s in (1, -1):
            later.append(send(piece(other, pair), piece(other, pair), to_y[s]))
        halves = []
        for n, s in enumerate((1, -1)):
            first[1 + n].wait_recv()
            view = part(row_at(0, -s), pair, n)
            halves.append(send(view, view, to_y[s]))
        return halves

    def spread_third(halves, pair):
        for n in range(2):
            halves[n].wait_recv()
            view = part(row_at(0, 2), pair, n)
            later.append(send(view, view, to_x))

    near_half = spread_second(near, xh)
    ql_core.wait_recv()
    ql_far.wait_recv()
    view = ql_all.at[z, 1 - xh, k]
    later.append(send(view, view, to_core))
    view = ql_all.at[z, :, k]
    ql_step = [send(view, view, to_z[s]) for s in (1, -1)]
    g_core.wait_recv()
    g_far.wait_recv()
    view = g_all.at[:, lanes(u_far, COLS)]
    later.append(send(view, view, to_core))

    def ql_forward(step, now):
        out = []
        for n, s in enumerate((1, -1)):
            now[n].wait_recv()
            owner = z_at(-s * step)
            view = ql_all.at[owner, :, k]
            if step < 3:
                out.append(send(view, view, to_z[s]))
            if step == 3:
                half = ql_all.at[owner, n, k]
                out.append(send(half, half, to_z[s]))
            if step == 4:
                view = ql_all.at[owner, n, k]
            later.append(send(view, view, to_core))
        return out

    far_half = spread_second(far, 1 - xh)
    ql_step = ql_forward(1, ql_step)
    spread_third(near_half, xh)
    ql_step = ql_forward(2, ql_step)
    spread_third(far_half, 1 - xh)
    ql_step = ql_forward(3, ql_step)
    ql_forward(4, ql_step)
    for copy in later:
        copy.wait_recv()

    def right_part(owner):
        return jnp.dot(
            g_all[...], qr_all[owner].reshape(4 * COLS, COLS), preferred_element_type=f32
        )

    cut = ROWS // 2
    halves = (pl.ds(0, cut), pl.ds(cut, cut))
    columns = (pl.ds(0, HALF), pl.ds(HALF, HALF))
    signs = (1, -1)
    term = right_part(z_at(4)).astype(bf16)
    moving = {}
    for n, s in enumerate(signs):
        p_send[n, 3, halves[n]] = term[n * cut : (n + 1) * cut]
    for h in range(2):
        for n, s in enumerate(signs):
            moving[n, h] = send(
                p_send.at[n, 3, halves[n], columns[h]],
                p_recv.at[n, 3, halves[n], columns[h]],
                to_z[s],
            )
    for stage in (3, 2, 1):
        for n, s in enumerate(signs):
            term = right_part(z_at(s * stage))
            for h in range(2):
                moving[n, h].wait_recv()
                lane = slice(h * HALF, (h + 1) * HALF)
                if stage == 3:
                    rows = slice(n * cut, (n + 1) * cut)
                    rest = slice((1 - n) * cut, (2 - n) * cut)
                    total = term[rows, lane] + p_recv[n, 3, halves[n], columns[h]].astype(f32)
                    p_send[n, 2, halves[n], columns[h]] = total.astype(bf16)
                    p_send[n, 2, halves[1 - n], columns[h]] = term[rest, lane].astype(bf16)
                else:
                    total = term[:, lane] + p_recv[n, stage, :, columns[h]].astype(f32)
                    p_send[n, stage - 1, :, columns[h]] = total.astype(bf16)
                moving[n, h] = send(
                    p_send.at[n, stage - 1, :, columns[h]],
                    p_recv.at[n, stage - 1, :, columns[h]],
                    to_z[s],
                )
    term = right_part(z)
    t_first = {}
    for h in range(2):
        for n in range(2):
            moving[n, h].wait_recv()
        total = term[:, h * HALF : (h + 1) * HALF]
        for n in range(2):
            total = total + p_recv[n, 0, :, columns[h]].astype(f32)
        t_all[row, :, columns[h]] = total.astype(bf16)
        t_first[h] = spread(lambda o: t_all.at[o, :, columns[h]], row)

    t_half, t_later = {}, {}
    for h in range(2):
        t_later[h] = []
        t_first[h][0].wait_recv()
        view = t_all.at[row_at(1, 0), :, columns[h]]
        for s in signs:
            t_later[h].append(send(view, view, to_y[s]))
        t_half[h] = []
        for n, s in enumerate(signs):
            t_first[h][1 + n].wait_recv()
            view = t_all.at[row_at(0, -s), halves[n], columns[h]]
            t_half[h].append(send(view, view, to_y[s]))
    for h in range(2):
        for n in range(2):
            t_half[h][n].wait_recv()
            view = t_all.at[row_at(0, 2), halves[n], columns[h]]
            t_later[h].append(send(view, view, to_x))

    def back_recv(slot, h, rows=slice(None)):
        return b_recv[slot, rows, columns[h]].astype(f32)

    def back_send(slot, h, value, to):
        b_send[slot, :, columns[h]] = value.astype(bf16)
        return send(b_send.at[slot, :, columns[h]], b_recv.at[slot, :, columns[h]], to)

    n8, n45, n67, n23, n1 = {}, {}, {}, {}, {}
    for h in range(2):
        for copy in t_later[h]:
            copy.wait_recv()
        rotated = jnp.zeros((ROWS, HALF), f32)
        for owner in range(8):
            rotated += lax.dot_general(
                ql_all[owner].reshape(ROWS, ROWS), t_all[owner, :, columns[h]],
                (((0,), (0,)), ((), ())), preferred_element_type=f32,
            )
        first = beta_first * moment_first[:, columns[h]] + (1.0 - beta_first) * rotated
        second = (
            beta_second * moment_second[:, columns[h]] + (1.0 - beta_second) * rotated * rotated
        )
        first_new[:, columns[h]] = first
        second_new[:, columns[h]] = second
        step = (
            first / correct_first / (jnp.sqrt(second / correct_second) + epsilon)
        ).astype(bf16)

        def back(owner):
            return jnp.dot(
                ql_all[owner].reshape(ROWS, ROWS), step, preferred_element_type=f32
            )

        n8[h] = back_send(0, h, back(row_at(1, 2)), to_x)
        n45[h] = [back_send(1 + n, h, back(row_at(1, s)), to_y[s]) for n, s in enumerate(signs)]
        for slot, owner in enumerate((row_at(0, 2), row_at(0, 1), row_at(0, -1), row_at(1, 0), row)):
            b_part[slot, :, columns[h]] = back(owner)
    for h in range(2):
        n8[h].wait_recv()
        total = b_part[0, :, columns[h]] + back_recv(0, h)
        b_send[3, :, columns[h]] = total.astype(bf16)
        n67[h] = [
            send(b_send.at[3, halves[n], columns[h]], b_recv.at[3, halves[n], columns[h]], to_y[-s])
            for n, s in enumerate(signs)
        ]
    for h in range(2):
        for n in range(2):
            n45[h][n].wait_recv()
        total = b_part[3, :, columns[h]] + back_recv(1, h) + back_recv(2, h)
        n1[h] = back_send(4, h, total, to_x)
        n23[h] = []
        for n, s in enumerate(signs):
            n67[h][1 - n].wait_recv()
            slot = 5 + n
            rows = halves[1 - n]
            total = b_part[1 + n, rows, columns[h]] + b_recv[3, rows, columns[h]].astype(f32)
            b_send[slot, rows, columns[h]] = total.astype(bf16)
            rows = halves[n]
            b_send[slot, rows, columns[h]] = b_part[1 + n, rows, columns[h]].astype(bf16)
            n23[h].append(
                send(b_send.at[slot, :, columns[h]], b_recv.at[slot, :, columns[h]], to_y[s])
            )
    e_step = {}
    for h in range(2):
        n1[h].wait_recv()
        for n in range(2):
            n23[h][n].wait_recv()
        total = b_part[4, :, columns[h]] + back_recv(4, h) + back_recv(5, h) + back_recv(6, h)
        b_all[z, :, columns[h]] = total.astype(bf16)
        view = b_all.at[z, :, columns[h]]
        for n, s in enumerate(signs):
            e_step[n, h] = send(view, view, to_z[s])

    def direction_part(owner, rows=slice(None)):
        return lax.dot_general(
            b_all[owner, rows], qr_all[owner].reshape(4 * COLS, COLS),
            (((1,), (1,)), ((), ())), preferred_element_type=f32,
        )

    d_acc[...] = direction_part(z)
    for stage in (1, 2, 3):
        for h in range(2):
            for n, s in enumerate(signs):
                e_step[n, h].wait_recv()
                owner = z_at(-s * stage)
                if stage < 3:
                    view = b_all.at[owner, :, columns[h]]
                else:
                    view = b_all.at[owner, halves[n], columns[h]]
                e_step[n, h] = send(view, view, to_z[s])
        for s in signs:
            d_acc[...] += direction_part(z_at(-s * stage))
    for n in range(2):
        for h in range(2):
            e_step[n, h].wait_recv()
        d_acc[halves[n]] += direction_part(z_at(4), halves[n])

    for m in range(2):
        d_send[m] = d_acc[:, lanes(2 * m + (1 - k), COLS)].astype(bf16)
    d_core = send(d_send.at[pl.ds(0, 2)], d_recv.at[pl.ds(0, 2)], to_core)
    d_core.wait_recv()
    total = d_acc[:, lanes(u_far, COLS)] + d_recv[1 - xh].astype(f32)
    d_send[2] = total.astype(bf16)
    d_far = send(d_send.at[2], d_recv.at[2], to_far)
    total = d_acc[:, lanes(u, COLS)] + d_recv[xh].astype(f32)
    d_far.wait_recv()
    direction = total + d_recv[2].astype(f32)
    update[...] = direction.astype(bf16)
    wide = weight[...].astype(f32)
    new_weight[...] = (wide - learn_rate * (direction + decay_rate * wide)).astype(bf16)
    for copy in started:
        copy.wait_send()


def on_device(weight, grad, moment_first, moment_second, basis_left, basis_right):
    block = (ROWS, COLS)
    vmem = pl.BlockSpec(memory_space=pltpu.VMEM)
    return pl.pallas_call(
        kernel,
        name="soap_step",
        out_shape=(
            jax.ShapeDtypeStruct(block, bf16),
            jax.ShapeDtypeStruct(block, bf16),
            jax.ShapeDtypeStruct(block, f32),
            jax.ShapeDtypeStruct(block, f32),
        ),
        in_specs=[vmem] * 6,
        out_specs=(vmem,) * 4,
        scratch_shapes=[
            pltpu.VMEM((8, 4, COLS, COLS), bf16),
            pltpu.VMEM((ROWS, 4 * COLS), bf16),
            pltpu.VMEM((8, 2, 2, 128, ROWS), bf16),
            pltpu.VMEM((8,) + block, bf16),
            pltpu.VMEM((2, 4) + block, bf16),
            pltpu.VMEM((2, 4) + block, bf16),
            pltpu.VMEM((5,) + block, f32),
            pltpu.VMEM((7,) + block, bf16),
            pltpu.VMEM((7,) + block, bf16),
            pltpu.VMEM((8,) + block, bf16),
            pltpu.VMEM((ROWS, 4 * COLS), f32),
            pltpu.VMEM((3,) + block, bf16),
            pltpu.VMEM((3,) + block, bf16),
            pltpu.SemaphoreType.DMA((N_MSG,)),
            pltpu.SemaphoreType.DMA((N_MSG,)),
        ],
        compiler_params=pltpu.CompilerParams(
            collective_id=0, has_side_effects=True, vmem_limit_bytes=56 * 2**20
        ),
        cost_estimate=pl.CostEstimate(
            flops=6 * 2**30, bytes_accessed=4 * 2**20, transcendentals=0
        ),
    )(weight, grad, moment_first, moment_second, basis_left, basis_right)


def solution(mesh):
    spec = P("row", "col")
    turned = P("col", "row")
    return jax.shard_map(
        on_device,
        mesh=mesh,
        in_specs=(spec, spec, spec, spec, turned, turned),
        out_specs=(spec,) * 4,
        check_vma=False,
    )
```

```python
import jax
import jax.numpy as jnp
from jax import lax
from jax.experimental import pallas as pl
from jax.experimental.pallas import tpu as pltpu
from jax.sharding import PartitionSpec as P

beta_first = 0.9
beta_second = 0.95
correct_first = 1.0 - 0.9**10
correct_second = 1.0 - 0.95**10
epsilon = 1e-08
learn_rate = 0.001
decay_rate = 0.1

ROWS = 512
COLS = 256
HALF = 128
N_MSG = 160

f32 = jnp.float32
bf16 = jnp.bfloat16


def kernel(
    weight, grad, moment_first, moment_second, ql, qr,
    new_weight, update, first_new, second_new,
    qr_all, g_all, ql_all, t_all, p_send, p_recv, b_part, b_send, b_recv, b_all,
    d_acc, d_send, d_recv, send_sem, recv_sem,
):
    row, col = lax.axis_index("row"), lax.axis_index("col")
    xl, y = lax.div(row, 4), lax.rem(row, 4)
    z, u = lax.div(col, 4), lax.rem(col, 4)
    xh, k = lax.div(u, 2), lax.rem(u, 2)

    def ring(value, shift, size):
        return lax.rem(value + (shift + size), size)

    u_core = xh * 2 + (1 - k)
    u_far = (1 - xh) * 2 + k
    u_cross = (1 - xh) * 2 + (1 - k)
    z_at = lambda s: ring(z, s, 8)
    row_at = lambda side, s: (xl if side == 0 else 1 - xl) * 4 + ring(y, s, 4)
    to_core = (row, z * 4 + u_core)
    to_far = (row, z * 4 + u_far)
    to_cross = (row, z * 4 + u_cross)
    to_z = {s: (row, z_at(s) * 4 + u) for s in (1, -1)}
    to_y = {s: (row_at(0, s), col) for s in (1, -1)}
    to_x = (row_at(1, 0), col)

    started = []

    def send(src, dst, to):
        n = len(started)
        copy = pltpu.make_async_remote_copy(
            src_ref=src, dst_ref=dst, send_sem=send_sem.at[n], recv_sem=recv_sem.at[n],
            device_id=to, device_id_type=pl.DeviceIdType.MESH,
        )
        copy.start()
        started.append(copy)
        return copy

    def lanes(index, width):
        return pl.ds(pl.multiple_of(index * width, width), width)

    barrier = pltpu.get_barrier_semaphore()
    partners = (to_core, to_far, to_cross, to_z[1], to_z[-1], to_y[1], to_y[-1], to_x)
    for partner in partners:
        pl.semaphore_signal(
            barrier, inc=1, device_id=partner, device_id_type=pl.DeviceIdType.MESH
        )
    pl.semaphore_wait(barrier, len(partners))

    near_in = send(qr.at[:, lanes(u_core, COLS)], qr_all.at[row, u], to_core)
    far_in = send(qr.at[:, lanes(u_far, COLS)], qr_all.at[row, u], to_far)
    cross_in = send(qr.at[:, lanes(u_cross, COLS)], qr_all.at[row, u], to_cross)
    ql_far = send(ql, ql_all.at[z, xh, k], to_far)
    ql_core = send(ql, ql_all.at[z, xh, k], to_core)
    g_core = send(grad, g_all.at[:, lanes(u, COLS)], to_core)
    qr_all[row, u] = qr[:, lanes(u, COLS)]
    g_all[:, lanes(u, COLS)] = grad[...]
    ql_all[z, xh, k] = ql[...]

    def spread(ref, owner):
        view = ref(owner)
        return [send(view, view, to_x), send(view, view, to_y[1]), send(view, view, to_y[-1])]

    def piece(pair):
        return lambda owner: qr_all.at[owner, pl.ds(pair * 2, 2)]

    def spread_other(first, ref):
        first[0].wait_recv()
        view = ref(row_at(1, 0))
        return [send(view, view, to_y[s]) for s in (1, -1)]

    def spread_half(first, ref):
        out = []
        for n, s in enumerate((1, -1)):
            first[1 + n].wait_recv()
            view = ref(row_at(0, -s), n)
            out.append(send(view, view, to_y[s]))
        return out

    def spread_last(half, ref):
        out = []
        for n in range(2):
            half[n].wait_recv()
            view = ref(row_at(0, 2), n)
            out.append(send(view, view, to_x))
        return out

    ql_later = []

    def ql_forward(step, now):
        out = []
        for n, s in enumerate((1, -1)):
            now[n].wait_recv()
            owner = z_at(-s * step)
            view = ql_all.at[owner, :, k]
            if step < 3:
                out.append(send(view, view, to_z[s]))
            if step == 3:
                half = ql_all.at[owner, n, k]
                out.append(send(half, half, to_z[s]))
            if step == 4:
                view = ql_all.at[owner, n, k]
            ql_later.append(send(view, view, to_core))
        return out

    def part(pair):
        return lambda owner, n: qr_all.at[owner, pair * 2 + n]

    near_in.wait_recv()
    near = spread(piece(xh), row)
    far_in.wait_recv()
    cross_in.wait_recv()
    far = spread(piece(1 - xh), row)
    g_far = send(grad, g_all.at[:, lanes(u, COLS)], to_far)
    near_half = spread_half(near, part(xh))
    ql_far.wait_recv()
    view = ql_all.at[z, 1 - xh, k]
    ql_later.append(send(view, view, to_core))
    view = ql_all.at[z, :, k]
    ql_step = [send(view, view, to_z[s]) for s in (1, -1)]
    far_half = spread_half(far, part(1 - xh))
    near_other = spread_other(near, piece(xh))
    ql_step = ql_forward(1, ql_step)
    near_last = spread_last(near_half, part(xh))
    far_other = spread_other(far, piece(1 - xh))
    far_last = spread_last(far_half, part(1 - xh))
    ql_step = ql_forward(2, ql_step)
    g_far.wait_recv()
    view = g_all.at[:, lanes(u_far, COLS)]
    g_cross = send(view, view, to_core)
    ql_step = ql_forward(3, ql_step)
    for copy in [g_core, g_cross] + near_other + far_other + near_last + far_last:
        copy.wait_recv()

    def right_part(owner):
        return jnp.dot(
            g_all[...], qr_all[owner].reshape(4 * COLS, COLS), preferred_element_type=f32
        )

    cut = ROWS // 2
    halves = (pl.ds(0, cut), pl.ds(cut, cut))
    columns = (pl.ds(0, HALF), pl.ds(HALF, HALF))
    signs = (1, -1)
    term = right_part(z_at(4)).astype(bf16)
    moving = {}
    for n, s in enumerate(signs):
        p_send[n, 3, halves[n]] = term[n * cut : (n + 1) * cut]
    for h in range(2):
        for n, s in enumerate(signs):
            moving[n, h] = send(
                p_send.at[n, 3, halves[n], columns[h]],
                p_recv.at[n, 3, halves[n], columns[h]],
                to_z[s],
            )
    for stage in (3, 2, 1):
        for n, s in enumerate(signs):
            term = right_part(z_at(s * stage))
            for h in range(2):
                moving[n, h].wait_recv()
                lane = slice(h * HALF, (h + 1) * HALF)
                if stage == 3:
                    rows = slice(n * cut, (n + 1) * cut)
                    rest = slice((1 - n) * cut, (2 - n) * cut)
                    total = term[rows, lane] + p_recv[n, 3, halves[n], columns[h]].astype(f32)
                    p_send[n, 2, halves[n], columns[h]] = total.astype(bf16)
                    p_send[n, 2, halves[1 - n], columns[h]] = term[rest, lane].astype(bf16)
                else:
                    total = term[:, lane] + p_recv[n, stage, :, columns[h]].astype(f32)
                    p_send[n, stage - 1, :, columns[h]] = total.astype(bf16)
                moving[n, h] = send(
                    p_send.at[n, stage - 1, :, columns[h]],
                    p_recv.at[n, stage - 1, :, columns[h]],
                    to_z[s],
                )
    term = right_part(z)
    t_first = {}
    for h in range(2):
        for n in range(2):
            moving[n, h].wait_recv()
        total = term[:, h * HALF : (h + 1) * HALF]
        for n in range(2):
            total = total + p_recv[n, 0, :, columns[h]].astype(f32)
        t_all[row, :, columns[h]] = total.astype(bf16)
        t_first[h] = spread(lambda o: t_all.at[o, :, columns[h]], row)

    ql_forward(4, ql_step)
    t_half, t_later = {}, {}
    for h in range(2):
        t_later[h] = []
        t_first[h][0].wait_recv()
        view = t_all.at[row_at(1, 0), :, columns[h]]
        for s in signs:
            t_later[h].append(send(view, view, to_y[s]))
        t_half[h] = []
        for n, s in enumerate(signs):
            t_first[h][1 + n].wait_recv()
            view = t_all.at[row_at(0, -s), halves[n], columns[h]]
            t_half[h].append(send(view, view, to_y[s]))
    for h in range(2):
        for n in range(2):
            t_half[h][n].wait_recv()
            view = t_all.at[row_at(0, 2), halves[n], columns[h]]
            t_later[h].append(send(view, view, to_x))

    def back_recv(slot, h, rows=slice(None)):
        return b_recv[slot, rows, columns[h]].astype(f32)

    def back_send(slot, h, value, to):
        b_send[slot, :, columns[h]] = value.astype(bf16)
        return send(b_send.at[slot, :, columns[h]], b_recv.at[slot, :, columns[h]], to)

    n8, n45, n67, n23, n1 = {}, {}, {}, {}, {}
    for copy in [ql_core] + ql_later:
        copy.wait_recv()
    for h in range(2):
        for copy in t_later[h]:
            copy.wait_recv()
        rotated = jnp.zeros((ROWS, HALF), f32)
        for owner in range(8):
            rotated += lax.dot_general(
                ql_all[owner].reshape(ROWS, ROWS), t_all[owner, :, columns[h]],
                (((0,), (0,)), ((), ())), preferred_element_type=f32,
            )
        first = beta_first * moment_first[:, columns[h]] + (1.0 - beta_first) * rotated
        second = (
            beta_second * moment_second[:, columns[h]] + (1.0 - beta_second) * rotated * rotated
        )
        first_new[:, columns[h]] = first
        second_new[:, columns[h]] = second
        step = (
            first / correct_first / (jnp.sqrt(second / correct_second) + epsilon)
        ).astype(bf16)

        def back(owner):
            return jnp.dot(
                ql_all[owner].reshape(ROWS, ROWS), step, preferred_element_type=f32
            )

        n8[h] = back_send(0, h, back(row_at(1, 2)), to_x)
        n45[h] = [back_send(1 + n, h, back(row_at(1, s)), to_y[s]) for n, s in enumerate(signs)]
        for slot, owner in enumerate((row_at(0, 2), row_at(0, 1), row_at(0, -1), row_at(1, 0), row)):
            b_part[slot, :, columns[h]] = back(owner)
    for h in range(2):
        n8[h].wait_recv()
        total = b_part[0, :, columns[h]] + back_recv(0, h)
        b_send[3, :, columns[h]] = total.astype(bf16)
        n67[h] = [
            send(b_send.at[3, halves[n], columns[h]], b_recv.at[3, halves[n], columns[h]], to_y[-s])
            for n, s in enumerate(signs)
        ]
    for h in range(2):
        for n in range(2):
            n45[h][n].wait_recv()
        total = b_part[3, :, columns[h]] + back_recv(1, h) + back_recv(2, h)
        n1[h] = back_send(4, h, total, to_x)
        n23[h] = []
        for n, s in enumerate(signs):
            n67[h][1 - n].wait_recv()
            slot = 5 + n
            rows = halves[1 - n]
            total = b_part[1 + n, rows, columns[h]] + b_recv[3, rows, columns[h]].astype(f32)
            b_send[slot, rows, columns[h]] = total.astype(bf16)
            rows = halves[n]
            b_send[slot, rows, columns[h]] = b_part[1 + n, rows, columns[h]].astype(bf16)
            n23[h].append(
                send(b_send.at[slot, :, columns[h]], b_recv.at[slot, :, columns[h]], to_y[s])
            )
    e_step = {}
    for h in range(2):
        n1[h].wait_recv()
        for n in range(2):
            n23[h][n].wait_recv()
        total = b_part[4, :, columns[h]] + back_recv(4, h) + back_recv(5, h) + back_recv(6, h)
        b_all[z, :, columns[h]] = total.astype(bf16)
        view = b_all.at[z, :, columns[h]]
        for n, s in enumerate(signs):
            e_step[n, h] = send(view, view, to_z[s])

    def direction_part(owner, rows=slice(None)):
        return lax.dot_general(
            b_all[owner, rows], qr_all[owner].reshape(4 * COLS, COLS),
            (((1,), (1,)), ((), ())), preferred_element_type=f32,
        )

    d_acc[...] = direction_part(z)
    for stage in (1, 2, 3):
        for h in range(2):
            for n, s in enumerate(signs):
                e_step[n, h].wait_recv()
                owner = z_at(-s * stage)
                if stage < 3:
                    view = b_all.at[owner, :, columns[h]]
                else:
                    view = b_all.at[owner, halves[n], columns[h]]
                e_step[n, h] = send(view, view, to_z[s])
        for s in signs:
            d_acc[...] += direction_part(z_at(-s * stage))
    for n in range(2):
        for h in range(2):
            e_step[n, h].wait_recv()
        d_acc[halves[n]] += direction_part(z_at(4), halves[n])

    for m in range(2):
        d_send[m] = d_acc[:, lanes(2 * m + (1 - k), COLS)].astype(bf16)
    d_core = send(d_send.at[pl.ds(0, 2)], d_recv.at[pl.ds(0, 2)], to_core)
    d_core.wait_recv()
    total = d_acc[:, lanes(u_far, COLS)] + d_recv[1 - xh].astype(f32)
    d_send[2] = total.astype(bf16)
    d_far = send(d_send.at[2], d_recv.at[2], to_far)
    total = d_acc[:, lanes(u, COLS)] + d_recv[xh].astype(f32)
    d_far.wait_recv()
    direction = total + d_recv[2].astype(f32)
    update[...] = direction.astype(bf16)
    wide = weight[...].astype(f32)
    new_weight[...] = (wide - learn_rate * (direction + decay_rate * wide)).astype(bf16)
    for copy in started:
        copy.wait_send()


def on_device(weight, grad, moment_first, moment_second, basis_left, basis_right):
    block = (ROWS, COLS)
    vmem = pl.BlockSpec(memory_space=pltpu.VMEM)
    return pl.pallas_call(
        kernel,
        name="soap_step",
        out_shape=(
            jax.ShapeDtypeStruct(block, bf16),
            jax.ShapeDtypeStruct(block, bf16),
            jax.ShapeDtypeStruct(block, f32),
            jax.ShapeDtypeStruct(block, f32),
        ),
        in_specs=[vmem] * 6,
        out_specs=(vmem,) * 4,
        scratch_shapes=[
            pltpu.VMEM((8, 4, COLS, COLS), bf16),
            pltpu.VMEM((ROWS, 4 * COLS), bf16),
            pltpu.VMEM((8, 2, 2, 128, ROWS), bf16),
            pltpu.VMEM((8,) + block, bf16),
            pltpu.VMEM((2, 4) + block, bf16),
            pltpu.VMEM((2, 4) + block, bf16),
            pltpu.VMEM((5,) + block, f32),
            pltpu.VMEM((7,) + block, bf16),
            pltpu.VMEM((7,) + block, bf16),
            pltpu.VMEM((8,) + block, bf16),
            pltpu.VMEM((ROWS, 4 * COLS), f32),
            pltpu.VMEM((3,) + block, bf16),
            pltpu.VMEM((3,) + block, bf16),
            pltpu.SemaphoreType.DMA((N_MSG,)),
            pltpu.SemaphoreType.DMA((N_MSG,)),
        ],
        compiler_params=pltpu.CompilerParams(
            collective_id=0, has_side_effects=True, vmem_limit_bytes=56 * 2**20
        ),
        cost_estimate=pl.CostEstimate(
            flops=6 * 2**30, bytes_accessed=4 * 2**20, transcendentals=0
        ),
    )(weight, grad, moment_first, moment_second, basis_left, basis_right)


def solution(mesh):
    spec = P("row", "col")
    turned = P("col", "row")
    return jax.shard_map(
        on_device,
        mesh=mesh,
        in_specs=(spec, spec, spec, spec, turned, turned),
        out_specs=(spec,) * 4,
        check_vma=False,
    )
```

```python
import jax
import jax.numpy as jnp
from jax import lax
from jax.experimental import pallas as pl
from jax.experimental.pallas import tpu as pltpu
from jax.sharding import PartitionSpec as P

beta_first = 0.9
beta_second = 0.95
correct_first = 1.0 - 0.9**10
correct_second = 1.0 - 0.95**10
epsilon = 1e-08
learn_rate = 0.001
decay_rate = 0.1

ROWS = 512
COLS = 256
HALF = 128
CUT = ROWS // 2
N_MSG = 256
SIGNS = (1, -1)
LANES = (pl.ds(0, HALF), pl.ds(HALF, HALF))
PARTS = (pl.ds(0, CUT), pl.ds(CUT, CUT))
ALL = pl.ds(0, ROWS)

f32 = jnp.float32
bf16 = jnp.bfloat16

RATE = {"core": 2.0e-6, "far": 22.3e-6, "x": 22.3e-6, "y": 22.3e-6, "z": 22.3e-6}
RANK = {"ql": 0.4, "g": 0.5}
for _h in range(2):
    for _kind in ("qr", "p", "t", "b", "e"):
        RANK[_kind, _h] = float(_h)
C_PARTS, D_PARTS = 2, 2
AHEAD = 1.5
DELAY = {"core": 1.0, "far": 3.7, "x": 2.2, "y": 2.2, "z": 2.2}


class Moving:
    def __init__(self, copy):
        self.copy, self.arrival, self.here = copy, None, False

    def wait(self):
        if not self.here:
            self.copy.wait_recv()
        self.here = True


class Task:
    def __init__(self, steps):
        self.steps, self.waits, self.done = steps, (), False


class Order:
    def __init__(self, send_sem, recv_sem):
        self.send_sem, self.recv_sem = send_sem, recv_sem
        self.now, self.free, self.queues = 0.0, {}, {}
        self.count, self.started, self.tasks = 0, [], []

    def send(self, src, dst, target, rank=0.0):
        to, link, side = target
        n = self.count
        self.count += 1
        copy = pltpu.make_async_remote_copy(
            src_ref=src, dst_ref=dst, send_sem=self.send_sem.at[n],
            recv_sem=self.recv_sem.at[n], device_id=to, device_id_type=pl.DeviceIdType.MESH,
        )
        size = 2
        for extent in dst.shape:
            size *= extent
        move = Moving(copy)
        key = ("x" if link == "far" else link, side)
        queue = self.queues.setdefault(key, [])
        queue.append((rank, n, link, size, move))
        if link == "core":
            self.issue(key)
        return move

    def issue(self, key):
        queue = self.queues[key]
        entry = min(queue, key=lambda item: item[:2])
        queue.remove(entry)
        link, size, move = entry[2:]
        move.copy.start()
        self.started.append(move.copy)
        self.free[key] = max(self.now, self.free.get(key, 0.0)) + size * RATE[link]
        move.arrival = self.free[key] + DELAY[link]

    def work(self, us):
        self.now += us

    def spawn(self, steps):
        task = Task(steps)
        self.tasks.append(task)
        self.step(task)
        return task

    def step(self, task):
        try:
            task.waits = next(task.steps)
        except StopIteration:
            task.done = True
            self.tasks.remove(task)

    def ready(self, task):
        time = 0.0
        for item in task.waits:
            if isinstance(item, Task):
                if not item.done:
                    return None
            elif item.arrival is None:
                return None
            else:
                time = max(time, item.arrival)
        return time

    def run(self):
        while self.tasks:
            events = []
            for n, task in enumerate(self.tasks):
                time = self.ready(task)
                if time is not None:
                    events.append((max(time, self.now), 1, time, n, task))
            for key, queue in self.queues.items():
                if queue:
                    time = max(self.now, self.free.get(key, 0.0) - AHEAD)
                    events.append((time, 0, 0.0, key, None))
            self.now, _, _, key, task = min(events, key=lambda event: event[:3])
            if task is None:
                self.issue(key)
                continue
            for item in task.waits:
                if isinstance(item, Moving):
                    item.wait()
            self.step(task)


def kernel(
    weight, grad, moment_first, moment_second, ql, qr,
    new_weight, update, first_new, second_new,
    qr_all, g_all, ql_all, t_all, r_acc, step_all, p_part, p_send, p_recv,
    b_part, b_send, b_recv, b_all, d_acc, d_send, d_recv, send_sem, recv_sem,
):
    row, col = lax.axis_index("row"), lax.axis_index("col")
    xl, y = lax.div(row, 4), lax.rem(row, 4)
    z, u = lax.div(col, 4), lax.rem(col, 4)
    xh, k = lax.div(u, 2), lax.rem(u, 2)

    def ring(value, shift, size):
        return lax.rem(value + (shift + size), size)

    def z_at(shift):
        return ring(z, shift, 8)

    def row_at(side, shift):
        return (xl if side == 0 else 1 - xl) * 4 + ring(y, shift, 4)

    u_core = xh * 2 + (1 - k)
    u_far = (1 - xh) * 2 + k
    u_cross = (1 - xh) * 2 + (1 - k)
    to_core = ((row, z * 4 + u_core), "core", 0)
    to_far = ((row, z * 4 + u_far), "far", 0)
    to_cross = ((row, z * 4 + u_cross), "far", 0)
    to_x = ((row_at(1, 0), col), "x", 0)
    to_y = {s: ((row_at(0, s), col), "y", s) for s in SIGNS}
    to_z = {s: ((row, z_at(s) * 4 + u), "z", s) for s in SIGNS}

    barrier = pltpu.get_barrier_semaphore()
    partners = (to_core, to_far, to_cross, to_z[1], to_z[-1], to_y[1], to_y[-1], to_x)
    for partner in partners:
        pl.semaphore_signal(
            barrier, inc=1, device_id=partner[0], device_id_type=pl.DeviceIdType.MESH
        )
    pl.semaphore_wait(barrier, len(partners))

    order = Order(send_sem, recv_sem)
    send, spawn, work = order.send, order.spawn, order.work

    def block(index, h=None):
        if h is None:
            return pl.ds(pl.multiple_of(index * COLS, COLS), COLS)
        return pl.ds(pl.multiple_of(index * COLS + h * HALF, HALF), HALF)

    def same(view, target, rank=0.0):
        return send(view, view, target, rank)

    def gather_row(full, half, arrived, rank, last_y=False):
        view = full(row)
        to_side = same(view, to_x, rank)
        first = [same(view, to_y[s], rank) for s in SIGNS]
        arrived(row, None)

        def side():
            yield [to_side]
            other = row_at(1, 0)
            view = full(other)
            copies = [same(view, to_y[s], rank) for s in SIGNS]
            arrived(other, None)
            for n, (copy, s) in enumerate(zip(copies, SIGNS)):
                yield [copy]
                arrived(row_at(1, -s), None)
                if last_y:
                    copies.append(same(half(row_at(1, -s), n), to_y[s], rank))
            for n, copy in enumerate(copies[2:]):
                yield [copy]
                arrived(row_at(1, 2), n)

        def along(n, s):
            yield [first[n]]
            view = half(row_at(0, -s), n)
            copy = same(view, to_y[s], rank)
            arrived(row_at(0, -s), None)
            yield [copy]
            if not last_y:
                view = half(row_at(0, 2), n)
                copy = same(view, to_x, rank)
            arrived(row_at(0, 2), n)
            if not last_y:
                yield [copy]
                arrived(row_at(1, 2), n)

        tasks = [spawn(along(n, s)) for n, s in enumerate(SIGNS)]
        return [spawn(side())] + tasks

    qr_tasks = {}

    def qr_pair(h, copies, pair, last_y=False):
        yield copies
        tasks = gather_row(
            lambda owner: qr_all.at[owner, pl.ds(pair * 2, 2), :, LANES[h]],
            lambda owner, n: qr_all.at[owner, pair * 2 + n, :, LANES[h]],
            lambda owner, n: None,
            RANK["qr", h],
            last_y,
        )
        yield tasks

    def qr_send(h, to_u, target):
        return send(qr.at[:, block(to_u, h)], qr_all.at[row, u, :, LANES[h]], target, RANK["qr", h])

    far = {}
    far[0] = [qr_send(0, u_far, to_far), qr_send(0, u_cross, to_cross)]
    near = [qr_send(h, u_core, to_core) for h in range(2)]
    ql_far = send(ql, ql_all.at[z, xh, k], to_far, RANK["ql"])
    far[1] = [qr_send(1, u_far, to_far), qr_send(1, u_cross, to_cross)]
    ql_core = send(ql, ql_all.at[z, xh, k], to_core)
    g_core = send(grad, g_all.at[:, block(u)], to_core)
    qr_all[row, u] = qr[:, block(u)]
    g_all[:, block(u)] = grad[...]
    ql_all[z, xh, k] = ql[...]

    def start_right():
        tasks = [spawn(qr_pair(0, [near[0]], xh))]
        tasks.append(spawn(qr_pair(0, far[0], 1 - xh, True)))
        g_far = [
            send(grad.at[rows], g_all.at[rows, block(u)], to_far, RANK["g"]) for rows in PARTS
        ]
        spawn(start_second())
        g_cross = []
        for copy, rows in zip(g_far, PARTS):
            yield [copy]
            g_cross.append(same(g_all.at[rows, block(u_far)], to_core))
        yield tasks + [g_core] + g_cross

    def start_second():
        qr_tasks[1] = [spawn(qr_pair(1, [near[1]], xh)), spawn(qr_pair(1, far[1], 1 - xh, True))]
        yield qr_tasks[1]

    ql_copies = [ql_core]

    def ql_chain(which):
        block_of = xh if which == 0 else 1 - xh
        if which == 1:
            yield [ql_far]
            ql_copies.append(same(ql_all.at[z, block_of, k], to_core))

        def along(n, s):
            move = same(ql_all.at[z, block_of, k], to_z[s], RANK["ql"])
            for step in (1, 2, 3, 4):
                if step == 4 and n != which:
                    break
                yield [move]
                view = ql_all.at[z_at(-s * step), block_of, k]
                if step < 3 or (step == 3 and n == which):
                    move = same(view, to_z[s], RANK["ql"])
                ql_copies.append(same(view, to_core))

        yield [spawn(along(n, s)) for n, s in enumerate(SIGNS)]

    def gather_left():
        yield [spawn(ql_chain(which)) for which in range(2)]
        yield ql_copies

    def right_part(owner, h):
        work(0.3)
        return jnp.dot(
            g_all[...], qr_all[owner, :, :, LANES[h]].reshape(4 * COLS, HALF),
            preferred_element_type=f32,
        )

    def sum_z(h):
        sends = {}

        def go(n, m, stage):
            return send(
                p_send.at[n, stage, PARTS[m], LANES[h]],
                p_recv.at[n, stage, PARTS[m], LANES[h]],
                to_z[SIGNS[n]],
                RANK["p", h],
            )

        term = right_part(z_at(4), h).astype(bf16)
        for n in range(2):
            p_send[n, 3, PARTS[n], LANES[h]] = term[n * CUT : (n + 1) * CUT]
            sends[n, n] = go(n, n, 3)
        for n, s in enumerate(SIGNS):
            term = right_part(z_at(3 * s), h)
            p_part[n, 3, :, LANES[h]] = term
            p_send[n, 2, PARTS[1 - n], LANES[h]] = term[(1 - n) * CUT : (2 - n) * CUT].astype(bf16)
            sends[n, 1 - n] = go(n, 1 - n, 2)
        for stage in (2, 1):
            for n, s in enumerate(SIGNS):
                p_part[n, stage, :, LANES[h]] = right_part(z_at(s * stage), h)
        p_part[0, 0, :, LANES[h]] = right_part(z, h)
        last = {}

        def along(n, m):
            move = sends[n, m]
            for stage in (3, 2, 1) if m == n else (2, 1):
                yield [move]
                total = p_part[n, stage, PARTS[m], LANES[h]]
                total = total + p_recv[n, stage, PARTS[m], LANES[h]].astype(f32)
                p_send[n, stage - 1, PARTS[m], LANES[h]] = total.astype(bf16)
                work(0.1)
                move = go(n, m, stage - 1)
            last[n, m] = move

        def arrive(m):
            yield chains[m]
            yield [last[n, m] for n in range(2)]
            total = p_part[0, 0, PARTS[m], LANES[h]]
            for n in range(2):
                total = total + p_recv[n, 0, PARTS[m], LANES[h]].astype(f32)
            t_all[row, PARTS[m], LANES[h]] = total.astype(bf16)
            work(0.1)

        chains = [[spawn(along(n, m)) for n in range(2)] for m in range(2)]
        b_done[h] = [spawn(arrive(m)) for m in range(2)]
        yield b_done[h] if C_PARTS == 1 else []

    def rotate(h, owner, first, size):
        work(0.05 + 0.15 * size / ROWS)
        r_acc[:, LANES[h]] += lax.dot_general(
            ql_all[owner].reshape(ROWS, ROWS)[first : first + size],
            t_all[owner, pl.ds(first, size), LANES[h]],
            (((0,), (0,)), ((), ())), preferred_element_type=f32,
        )

    def gather_rotate(h):
        r_acc[:, LANES[h]] = jnp.zeros((ROWS, HALF), f32)
        size = ROWS // C_PARTS
        waiting = []

        def put(owner, first, size):
            if left_task.done:
                rotate(h, owner, first, size)
            else:
                waiting.append((owner, first, size))

        def part(m):
            if C_PARTS == 2:
                yield [b_done[h][m]]

            def arrived(owner, n):
                if n is None:
                    put(owner, m * size, size)
                else:
                    put(owner, m * size + n * (size // 2), size // 2)

            yield gather_row(
                lambda owner: t_all.at[owner, pl.ds(m * size, size), LANES[h]],
                lambda owner, n: t_all.at[
                    owner, pl.ds(m * size + n * (size // 2), size // 2), LANES[h]
                ],
                arrived,
                RANK["t", h],
            )

        tasks = [spawn(part(m)) for m in range(C_PARTS)]
        yield [left_task]
        for item in waiting:
            rotate(h, *item)
        waiting.clear()
        yield tasks

    def sum_row(h):
        rotated = r_acc[:, LANES[h]]
        first = beta_first * moment_first[:, LANES[h]] + (1.0 - beta_first) * rotated
        second = (
            beta_second * moment_second[:, LANES[h]] + (1.0 - beta_second) * rotated * rotated
        )
        first_new[:, LANES[h]] = first
        second_new[:, LANES[h]] = second
        step_all[:, LANES[h]] = (
            first / correct_first / (jnp.sqrt(second / correct_second) + epsilon)
        ).astype(bf16)
        work(0.3)

        size = ROWS // D_PARTS

        def back(owner, m):
            work(0.25 / D_PARTS)
            return jnp.dot(
                ql_all[owner].reshape(ROWS, ROWS)[m * size : (m + 1) * size],
                step_all[:, LANES[h]],
                preferred_element_type=f32,
            )

        def came(slot, rows):
            return b_recv[slot, rows, LANES[h]].astype(f32)

        def own(slot, rows):
            return b_part[slot, rows, LANES[h]]

        def go(slot, target, rows):
            return send(
                b_send.at[slot, rows, LANES[h]], b_recv.at[slot, rows, LANES[h]], target,
                RANK["b", h],
            )

        spans = [pl.ds(m * size, size) for m in range(D_PARTS)]
        opposite, side = [], []
        for m in range(D_PARTS):
            b_send[0, spans[m], LANES[h]] = back(row_at(1, 2), m).astype(bf16)
            opposite.append(go(0, to_x, spans[m]))
        for m in range(D_PARTS):
            side.append([])
            for n, s in enumerate(SIGNS):
                b_send[1 + n, spans[m], LANES[h]] = back(row_at(1, s), m).astype(bf16)
                side[m].append(go(1 + n, to_y[s], spans[m]))
        owners = (row_at(0, 2), row_at(0, 1), row_at(0, -1), row_at(1, 0), row)
        for slot, owner in enumerate(owners):
            for m in range(D_PARTS):
                b_part[slot, spans[m], LANES[h]] = back(owner, m)

        def reduce(m):
            last, after = [], []
            pieces = [pl.ds(m * size + n * (size // 2), size // 2) for n in range(2)]

            def across():
                yield [opposite[m]]
                total = own(0, spans[m]) + came(0, spans[m])
                b_send[3, spans[m], LANES[h]] = total.astype(bf16)
                work(0.1)
                turned = [go(3, to_y[-s], pieces[n]) for n, s in enumerate(SIGNS)]
                for n, s in enumerate(SIGNS):
                    after.append(spawn(along(n, s, turned[1 - n])))

            def along(n, s, move):
                yield [move]
                rows, rest = pieces[1 - n], pieces[n]
                total = own(1 + n, rows) + came(3, rows)
                b_send[5 + n, rows, LANES[h]] = total.astype(bf16)
                b_send[5 + n, rest, LANES[h]] = own(1 + n, rest).astype(bf16)
                work(0.1)
                last.append(go(5 + n, to_y[s], spans[m]))

            def beside():
                yield side[m]
                total = own(3, spans[m]) + came(1, spans[m]) + came(2, spans[m])
                b_send[4, spans[m], LANES[h]] = total.astype(bf16)
                work(0.1)
                last.append(go(4, to_x, spans[m]))

            yield [spawn(across()), spawn(beside())]
            yield after
            yield last
            total = own(4, spans[m])
            for slot in (4, 5, 6):
                total = total + came(slot, spans[m])
            b_all[z, spans[m], LANES[h]] = total.astype(bf16)
            work(0.1)

        d_done[h] = [spawn(reduce(m)) for m in range(D_PARTS)]
        yield d_done[h] if D_PARTS == 1 else []

    def direction_part(owner, rows):
        work(0.4 if rows is ALL else 0.2)
        return lax.dot_general(
            b_all[owner, rows], qr_all[owner].reshape(4 * COLS, COLS),
            (((1,), (1,)), ((), ())), preferred_element_type=f32,
        )

    b_done, d_done = {}, {}
    seen = set()
    final = {}

    def add_direction(owner, what):
        if what in seen:
            if what == 0:
                d_acc[...] = direction_part(owner, ALL)
                seen.add("own")
            else:
                assert "own" in seen
                d_acc[...] += direction_part(owner, ALL)
        seen.add(what)

    def gather_z(h):
        count = {}

        def come(owner, what):
            count[what] = count.get(what, 0) + 1
            if count[what] == 2:
                add_direction(owner, what)

        def along(n, m):
            if D_PARTS == 2:
                yield [d_done[h][m]]
            s = SIGNS[n]
            if n == 0:
                come(z, 0)
            view = b_all.at[z, PARTS[m], LANES[h]]
            move = same(view, to_z[s], RANK["e", h])
            for stage in (1, 2, 3):
                yield [move]
                owner = z_at(-s * stage)
                if stage < 3 or m == n:
                    view = b_all.at[owner, PARTS[m], LANES[h]]
                    move = same(view, to_z[s], RANK["e", h])
                come(owner, (n, stage))
            if m == n:
                final[h, n] = move

        yield [spawn(along(n, m)) for m in range(2) for n in range(2)]

    def pipeline(h):
        yield [right_task]
        if h == 1:
            yield qr_tasks[1]
        for part in (sum_z, gather_rotate, sum_row, gather_z):
            yield [spawn(part(h))]

    def finish(a):
        rows = PARTS[a]
        yield pipelines
        yield [final[0, a], final[1, a]]
        d_acc[rows] += direction_part(z_at(4), rows)
        for m in range(2):
            d_send[m, rows] = d_acc[rows, block(2 * m + (1 - k))].astype(bf16)
        core = send(d_send.at[pl.ds(0, 2), rows], d_recv.at[pl.ds(0, 2), rows], to_core)
        yield [core]
        total = d_acc[rows, block(u_far)] + d_recv[1 - xh, rows].astype(f32)
        d_send[2, rows] = total.astype(bf16)
        far_copy = send(d_send.at[2, rows], d_recv.at[2, rows], to_far)
        yield [far_copy]
        total = d_acc[rows, block(u)] + d_recv[xh, rows].astype(f32)
        direction = total + d_recv[2, rows].astype(f32)
        update[rows] = direction.astype(bf16)
        wide = weight[rows].astype(f32)
        new_weight[rows] = (wide - learn_rate * (direction + decay_rate * wide)).astype(bf16)

    left_task = spawn(gather_left())
    right_task = spawn(start_right())
    pipelines = [spawn(pipeline(h)) for h in range(2)]
    for a in range(2):
        spawn(finish(a))
    order.run()
    for copy in order.started:
        copy.wait_send()


def on_device(weight, grad, moment_first, moment_second, basis_left, basis_right):
    block = (ROWS, COLS)
    vmem = pl.BlockSpec(memory_space=pltpu.VMEM)
    return pl.pallas_call(
        kernel,
        name="soap_step",
        out_shape=(
            jax.ShapeDtypeStruct(block, bf16),
            jax.ShapeDtypeStruct(block, bf16),
            jax.ShapeDtypeStruct(block, f32),
            jax.ShapeDtypeStruct(block, f32),
        ),
        in_specs=[vmem] * 6,
        out_specs=(vmem,) * 4,
        scratch_shapes=[
            pltpu.VMEM((8, 4, COLS, COLS), bf16),
            pltpu.VMEM((ROWS, 4 * COLS), bf16),
            pltpu.VMEM((8, 2, 2, 128, ROWS), bf16),
            pltpu.VMEM((8,) + block, bf16),
            pltpu.VMEM(block, f32),
            pltpu.VMEM(block, bf16),
            pltpu.VMEM((2, 4) + block, f32),
            pltpu.VMEM((2, 4) + block, bf16),
            pltpu.VMEM((2, 4) + block, bf16),
            pltpu.VMEM((5,) + block, f32),
            pltpu.VMEM((7,) + block, bf16),
            pltpu.VMEM((7,) + block, bf16),
            pltpu.VMEM((8,) + block, bf16),
            pltpu.VMEM((ROWS, 4 * COLS), f32),
            pltpu.VMEM((3,) + block, bf16),
            pltpu.VMEM((3,) + block, bf16),
            pltpu.SemaphoreType.DMA((N_MSG,)),
            pltpu.SemaphoreType.DMA((N_MSG,)),
        ],
        compiler_params=pltpu.CompilerParams(
            collective_id=0, has_side_effects=True, vmem_limit_bytes=56 * 2**20
        ),
        cost_estimate=pl.CostEstimate(
            flops=6 * 2**30, bytes_accessed=4 * 2**20, transcendentals=0
        ),
    )(weight, grad, moment_first, moment_second, basis_left, basis_right)


def solution(mesh):
    spec = P("row", "col")
    turned = P("col", "row")
    return jax.shard_map(
        on_device,
        mesh=mesh,
        in_specs=(spec, spec, spec, spec, turned, turned),
        out_specs=(spec,) * 4,
        check_vma=False,
    )
```

```python
import jax
import jax.numpy as jnp
from jax import lax
from jax.experimental import pallas as pl
from jax.experimental.pallas import tpu as pltpu
from jax.sharding import PartitionSpec as P

beta_first = 0.9
beta_second = 0.95
correct_first = 1.0 - 0.9**10
correct_second = 1.0 - 0.95**10
epsilon = 1e-08
learn_rate = 0.001
decay_rate = 0.1

ROWS = 512
COLS = 256
HALF = 128
CUT = ROWS // 2
N_MSG = 300
SIGNS = (1, -1)
LANES = (pl.ds(0, HALF), pl.ds(HALF, HALF))
PARTS = (pl.ds(0, CUT), pl.ds(CUT, CUT))
ALL = pl.ds(0, ROWS)

f32 = jnp.float32
bf16 = jnp.bfloat16

RATE = {"core": 2.0e-6, "far": 22.3e-6, "x": 22.3e-6, "o": 22.3e-6, "y": 22.3e-6, "z": 22.3e-6}
RANK = {
    ("b", 0, 0, 0): -0.18, ("b", 0, 0, 1): -0.65, ("b", 0, 0, 2): -0.39, ("b", 0, 0, 3): -0.91,
    ("b", 0, 0, 4): 0.67, ("b", 0, 0, 5): -0.92, ("b", 0, 0, 6): 0.98, ("b", 0, 1, 0): 0.16,
    ("b", 0, 1, 1): 0.81, ("b", 0, 1, 2): -0.06, ("b", 0, 1, 3): 1.51, ("b", 0, 1, 4): -1.33,
    ("b", 0, 1, 5): 1.19, ("b", 0, 1, 6): -0.62, ("b", 1, 0, 0): 0.32, ("b", 1, 0, 1): 1.55,
    ("b", 1, 0, 2): -2.48, ("b", 1, 0, 3): 2.07, ("b", 1, 0, 4): 1.13, ("b", 1, 0, 5): -0.97,
    ("b", 1, 0, 6): -0.87, ("b", 1, 1, 0): -1.47, ("b", 1, 1, 1): -0.04, ("b", 1, 1, 2): 0.2,
    ("b", 1, 1, 3): 1.23, ("b", 1, 1, 4): 1.88, ("b", 1, 1, 5): 0.01, ("b", 1, 1, 6): 1.46,
    ("e", 0, 0, 0): 1.54, ("e", 0, 0, 1): 1.16, ("e", 0, 0, 2): 0.74, ("e", 0, 0, 3): 1.72,
    ("e", 0, 1, 0): 1.51, ("e", 0, 1, 1): 1.48, ("e", 0, 1, 2): 0.56, ("e", 0, 1, 3): 1.21,
    ("e", 1, 0, 0): 0.6, ("e", 1, 0, 1): -1.51, ("e", 1, 0, 2): 1.5, ("e", 1, 0, 3): 0.68,
    ("e", 1, 1, 0): -0.72, ("e", 1, 1, 1): 1.3, ("e", 1, 1, 2): -1.36, ("e", 1, 1, 3): 1.4,
    ("g", 0): 1.9, ("g", 1): 1.66, ("in", 0, 1): 1.24, ("in", 0, 2): -0.35, ("in", 0, 3): -0.51,
    ("in", 1, 1): -0.25, ("in", 1, 2): 1.17, ("in", 1, 3): 0.87, ("p", 0, False, 0): 0.24,
    ("p", 0, False, 1): 0.17, ("p", 0, False, 2): 1.9, ("p", 0, True, 0): 0.04,
    ("p", 0, True, 1): -0.44, ("p", 0, True, 2): 0.56, ("p", 0, True, 3): 0.71,
    ("p", 1, False, 0): 1.38, ("p", 1, False, 1): -0.52, ("p", 1, False, 2): -0.31,
    ("p", 1, True, 0): 0.13, ("p", 1, True, 1): -1.84, ("p", 1, True, 2): -0.28,
    ("p", 1, True, 3): -0.71, ("ql", "far"): 1.1, ("ql", 0, 0): 0.26, ("ql", 0, 1): 0.35,
    ("ql", 0, 2): -0.36, ("ql", 0, 3): 0.14, ("ql", 1, 0): 1.57, ("ql", 1, 1): -0.3,
    ("ql", 1, 2): 0.35, ("ql", 1, 3): -0.01, ("qr", 0, 0, "half"): -0.0,
    ("qr", 0, 0, "last"): 2.11, ("qr", 0, 0, "other"): -0.37, ("qr", 0, 0, "x"): 1.32,
    ("qr", 0, 0, "y"): 2.12, ("qr", 0, 1, "half"): -0.48, ("qr", 0, 1, "last"): -0.36,
    ("qr", 0, 1, "other"): 1.89, ("qr", 0, 1, "x"): -0.92, ("qr", 0, 1, "y"): -0.3,
    ("qr", 0, 2, "half"): 1.42, ("qr", 0, 2, "last"): 2.57, ("qr", 0, 2, "other"): 0.41,
    ("qr", 0, 2, "x"): 0.3, ("qr", 0, 2, "y"): -1.32, ("qr", 0, 3, "half"): -0.09,
    ("qr", 0, 3, "last"): 1.18, ("qr", 0, 3, "other"): 1.24, ("qr", 0, 3, "x"): -1.07,
    ("qr", 0, 3, "y"): -1.71, ("qr", 1, 0, "half"): 7.28, ("qr", 1, 0, "last"): -1.82,
    ("qr", 1, 0, "other"): 1.17, ("qr", 1, 0, "x"): 7.28, ("qr", 1, 0, "y"): -0.79,
    ("qr", 1, 1, "half"): 7.42, ("qr", 1, 1, "last"): 1.45, ("qr", 1, 1, "other"): -0.13,
    ("qr", 1, 1, "x"): 6.0, ("qr", 1, 1, "y"): 2.65, ("qr", 1, 2, "half"): -1.43,
    ("qr", 1, 2, "last"): 2.51, ("qr", 1, 2, "other"): 0.5, ("qr", 1, 2, "x"): 11.2,
    ("qr", 1, 2, "y"): 7.65, ("qr", 1, 3, "half"): 2.25, ("qr", 1, 3, "last"): 0.65,
    ("qr", 1, 3, "other"): -0.04, ("qr", 1, 3, "x"): 13.6, ("qr", 1, 3, "y"): 6.81,
    ("t", 0, 0, "half"): 0.18, ("t", 0, 0, "last"): -1.08, ("t", 0, 0, "other"): 0.69,
    ("t", 0, 0, "x"): -0.17, ("t", 0, 0, "y"): 0.09, ("t", 0, 1, "half"): 0.94,
    ("t", 0, 1, "last"): -0.66, ("t", 0, 1, "other"): -0.03, ("t", 0, 1, "x"): -1.31,
    ("t", 0, 1, "y"): 0.58, ("t", 1, 0, "half"): 0.24, ("t", 1, 0, "last"): 1.46,
    ("t", 1, 0, "other"): 3.9, ("t", 1, 0, "x"): 2.96, ("t", 1, 0, "y"): 3.43,
    ("t", 1, 1, "half"): 2.67, ("t", 1, 1, "last"): 1.27, ("t", 1, 1, "other"): 1.79,
    ("t", 1, 1, "x"): 2.08, ("t", 1, 1, "y"): 0.27,
}


def rank_of(*key):
    if key in RANK:
        return RANK[key]
    if key[0] in ("ql", "g"):
        return 0.45
    return float(key[1])


LAST_Y = {("qr", 0, 2), ("t", 0, 0), ("t", 0, 1), ("t", 1, 1)}
C_PARTS, D_PARTS = 2, 2
Z_PARTS = 2
ZPARTS = [pl.ds(m * (ROWS // Z_PARTS), ROWS // Z_PARTS) for m in range(Z_PARTS)]
AHEAD = 1.5
DELAY = {"core": 1.0, "far": 3.7, "x": 2.2, "o": 2.2, "y": 2.2, "z": 2.2}


def new_moments(first, second, rotated):
    return (
        beta_first * first + (1.0 - beta_first) * rotated,
        beta_second * second + (1.0 - beta_second) * rotated * rotated,
    )


class Moving:
    def __init__(self, copy):
        self.copy, self.arrival, self.here = copy, None, False

    def wait(self):
        if not self.here:
            self.copy.wait_recv()
        self.here = True


class Task:
    def __init__(self, steps):
        self.steps, self.waits, self.done = steps, (), False


class Order:
    def __init__(self, send_sem, recv_sem):
        self.send_sem, self.recv_sem = send_sem, recv_sem
        self.now, self.free, self.queues = 0.0, {}, {}
        self.count, self.started, self.tasks = 0, [], []

    def send(self, src, dst, target, *key):
        to, link, side = target
        rank = rank_of(*key) if key else 0.0
        n = self.count
        self.count += 1
        copy = pltpu.make_async_remote_copy(
            src_ref=src, dst_ref=dst, send_sem=self.send_sem.at[n],
            recv_sem=self.recv_sem.at[n], device_id=to, device_id_type=pl.DeviceIdType.MESH,
        )
        size = 2
        for extent in dst.shape:
            size *= extent
        move = Moving(copy)
        key = ("x" if link == "far" else link, side)
        queue = self.queues.setdefault(key, [])
        queue.append((rank, n, link, size, move))
        if link == "core":
            self.issue(key)
        return move

    def issue(self, key):
        queue = self.queues[key]
        entry = min(queue, key=lambda item: item[:2])
        queue.remove(entry)
        link, size, move = entry[2:]
        move.copy.start()
        self.now += 0.05
        self.started.append(move.copy)
        self.free[key] = max(self.now, self.free.get(key, 0.0)) + size * RATE[link]
        move.arrival = self.free[key] + DELAY[link]

    def work(self, us):
        self.now += us

    def spawn(self, steps):
        task = Task(steps)
        self.tasks.append(task)
        self.step(task)
        return task

    def step(self, task):
        try:
            task.waits = next(task.steps)
        except StopIteration:
            task.done = True
            self.tasks.remove(task)

    def ready(self, task):
        time = 0.0
        for item in task.waits:
            if isinstance(item, Task):
                if not item.done:
                    return None
            elif item.arrival is None:
                return None
            else:
                time = max(time, item.arrival)
        return time

    def run(self):
        while self.tasks:
            events = []
            for n, task in enumerate(self.tasks):
                time = self.ready(task)
                if time is not None:
                    events.append((max(time, self.now), 1, time, n, task))
            for key, queue in self.queues.items():
                if queue:
                    time = max(self.now, self.free.get(key, 0.0) - AHEAD)
                    events.append((time, 0, 0.0, key, None))
            self.now, _, _, key, task = min(events, key=lambda event: event[:3])
            if task is None:
                self.issue(key)
                continue
            for item in task.waits:
                if isinstance(item, Moving):
                    item.wait()
            self.step(task)


def far_part(n, m):
    return m * 2 // Z_PARTS == n


def kernel(
    grad, moment_first, moment_second, ql, qr, rotated_out, direction_out,
    first_old, second_old, qr_all, g_all, ql_all, t_all, r_acc, step_all, p_part, p_send, p_recv,
    b_part, b_send, b_recv, b_all, d_acc, d_out, d_send, d_recv,
    send_sem, recv_sem, local_sem,
):
    row, col = lax.axis_index("row"), lax.axis_index("col")
    xl, y = lax.div(row, 4), lax.rem(row, 4)
    z, u = lax.div(col, 4), lax.rem(col, 4)
    xh, k = lax.div(u, 2), lax.rem(u, 2)

    def ring(value, shift, size):
        return lax.rem(value + (shift + size), size)

    def z_at(shift):
        return ring(z, shift, 8)

    def row_at(side, shift):
        return (xl if side == 0 else 1 - xl) * 4 + ring(y, shift, 4)

    u_core = xh * 2 + (1 - k)
    u_far = (1 - xh) * 2 + k
    u_cross = (1 - xh) * 2 + (1 - k)
    to_core = ((row, z * 4 + u_core), "core", 0)
    to_far = ((row, z * 4 + u_far), "far", 0)
    to_x = ((row_at(1, 0), col), "x", 0)
    to_other = ((row_at(1, 0), z * 4 + u_far), "o", 0)
    to_cross = ((row_at(1, 0), z * 4 + u_cross), "o", 0)
    to_y = {s: ((row_at(0, s), col), "y", s) for s in SIGNS}
    to_z = {s: ((row, z_at(s) * 4 + u), "z", s) for s in SIGNS}

    def block(index, h=None):
        if h is None:
            return pl.ds(pl.multiple_of(index * COLS, COLS), COLS)
        return pl.ds(pl.multiple_of(index * COLS + h * HALF, HALF), HALF)

    barrier = pltpu.get_barrier_semaphore()
    partners = (to_core, to_far, to_other, to_cross, to_z[1], to_z[-1], to_y[1], to_y[-1], to_x)
    for partner in partners:
        pl.semaphore_signal(
            barrier, inc=1, device_id=partner[0], device_id_type=pl.DeviceIdType.MESH
        )
    local = []

    def move(src, dst):
        copy = pltpu.make_async_copy(src, dst, local_sem.at[len(local)])
        copy.start()
        local.append(copy)
        return copy

    own_copies = [move(qr.at[:, block(u, h)], qr_all.at[h, row, u]) for h in range(2)]
    own_copies.append(move(ql, ql_all.at[z, xh, k]))
    own_copies.append(move(grad, g_all.at[:, block(u)]))
    old_copies = [move(moment_first, first_old), move(moment_second, second_old)]
    pl.semaphore_wait(barrier, len(partners))

    order = Order(send_sem, recv_sem)
    send, spawn, work = order.send, order.spawn, order.work

    def same(view, target, *key):
        return send(view, view, target, *key)

    def gather_row(full, half, arrived, flip, *key):
        last_y = key in LAST_Y

        def at(side, shift):
            return row_at(side if not flip else 1 - side, shift)

        view = full(at(0, 0))
        to_side = same(view, to_x, *key, "x")
        first = [same(view, to_y[s], *key, "y") for s in SIGNS]
        arrived(at(0, 0), None)

        def side():
            yield [to_side]
            other = at(1, 0)
            view = full(other)
            copies = [same(view, to_y[s], *key, "other") for s in SIGNS]
            arrived(other, None)
            for n, (copy, s) in enumerate(zip(copies, SIGNS)):
                yield [copy]
                arrived(at(1, -s), None)
                if last_y:
                    copies.append(same(half(at(1, -s), n), to_y[s], *key, "last"))
            for n, copy in enumerate(copies[2:]):
                yield [copy]
                arrived(at(1, 2), n)

        def along(n, s):
            yield [first[n]]
            view = half(at(0, -s), n)
            copy = same(view, to_y[s], *key, "half")
            arrived(at(0, -s), None)
            yield [copy]
            if not last_y:
                view = half(at(0, 2), n)
                copy = same(view, to_x, *key, "last")
            arrived(at(0, 2), n)
            if not last_y:
                yield [copy]
                arrived(at(1, 2), n)

        tasks = [spawn(along(n, s)) for n, s in enumerate(SIGNS)]
        return [spawn(side())] + tasks

    blocks = (u, u_core, u_far, u_cross)

    def qr_block(h, i):
        if i > 0:
            yield [qr_in[h, i]]
        source = blocks[i]
        yield gather_row(
            lambda owner: qr_all.at[h, owner, source, :],
            lambda owner, n: qr_all.at[h, owner, source, pl.ds(n * HALF, HALF)],
            lambda owner, n: None,
            i > 1,
            "qr", h, i,
        )

    qr_in = {}
    for h in range(2):
        for i, target in ((1, to_core), (2, to_other), (3, to_cross)):
            qr_in[h, i] = send(
                qr.at[:, block(blocks[i], h)], qr_all.at[h, row, u, :], target,
                "in", h, i,
            )
    ql_far = send(ql, ql_all.at[z, xh, k], to_far, "ql", "far")
    g_far = [
        send(grad.at[rows], g_all.at[rows, block(u)], to_far, "g", n)
        for n, rows in enumerate(PARTS)
    ]
    ql_core = send(ql, ql_all.at[z, xh, k], to_core)
    g_core = send(grad, g_all.at[:, block(u)], to_core)
    for copy in own_copies + old_copies:
        copy.wait()

    def gather_right(h):
        yield [spawn(qr_block(h, i)) for i in range(4)]

    def gather_grad():
        g_cross = []
        for copy, rows in zip(g_far, PARTS):
            yield [copy]
            g_cross.append(same(g_all.at[rows, block(u_far)], to_core))
        yield [g_core] + g_cross

    ql_copies = [ql_core]

    def ql_chain(which):
        block_of = xh if which == 0 else 1 - xh
        if which == 1:
            yield [ql_far]
            ql_copies.append(same(ql_all.at[z, block_of, k], to_core))

        def along(n, s):
            move = same(ql_all.at[z, block_of, k], to_z[s], "ql", which, 0)
            for step in (1, 2, 3, 4):
                if step == 4 and n != which:
                    break
                yield [move]
                view = ql_all.at[z_at(-s * step), block_of, k]
                if step < 3 or (step == 3 and n == which):
                    move = same(view, to_z[s], "ql", which, step)
                ql_copies.append(same(view, to_core))

        yield [spawn(along(n, s)) for n, s in enumerate(SIGNS)]

    def gather_left():
        yield [spawn(ql_chain(which)) for which in range(2)]
        yield ql_copies

    def right_part(owner, h):
        work(0.3)
        return jnp.dot(
            g_all[...], qr_all[h, owner, :, :].reshape(4 * COLS, HALF),
            preferred_element_type=f32,
        )

    def sum_z(h):
        sends = {}

        def go(n, m, stage):
            return send(
                p_send.at[h, n, stage, ZPARTS[m]],
                p_recv.at[h, n, stage, ZPARTS[m]],
                to_z[SIGNS[n]],
                "p", h, far_part(n, m), stage,
            )

        term = right_part(z_at(4), h).astype(bf16)
        p_send[h, 0, 3, PARTS[0]] = term[:CUT]
        p_send[h, 1, 3, PARTS[1]] = term[CUT:]
        for m in range(Z_PARTS):
            n = 0 if far_part(0, m) else 1
            sends[n, m] = go(n, m, 3)
        for n, s in enumerate(SIGNS):
            term = right_part(z_at(3 * s), h)
            p_part[h, n, 3, :] = term
            p_send[h, n, 2, PARTS[1 - n]] = term[(1 - n) * CUT : (2 - n) * CUT].astype(bf16)
            for m in range(Z_PARTS):
                if not far_part(n, m):
                    sends[n, m] = go(n, m, 2)
        for stage in (2, 1):
            for n, s in enumerate(SIGNS):
                p_part[h, n, stage, :] = right_part(z_at(s * stage), h)
        p_part[h, 0, 0, :] = right_part(z, h)
        last = {}

        def along(n, m):
            move = sends[n, m]
            for stage in (3, 2, 1) if far_part(n, m) else (2, 1):
                yield [move]
                total = p_part[h, n, stage, ZPARTS[m]]
                total = total + p_recv[h, n, stage, ZPARTS[m]].astype(f32)
                p_send[h, n, stage - 1, ZPARTS[m]] = total.astype(bf16)
                work(0.2 / Z_PARTS)
                move = go(n, m, stage - 1)
            last[n, m] = move

        def arrive(c):
            parts = range(c * Z_PARTS // 2, (c + 1) * Z_PARTS // 2)
            for m in parts:
                yield chains[m]
                yield [last[n, m] for n in range(2)]
                total = p_part[h, 0, 0, ZPARTS[m]]
                for n in range(2):
                    total = total + p_recv[h, n, 0, ZPARTS[m]].astype(f32)
                t_all[h, row, ZPARTS[m]] = total.astype(bf16)
                work(0.2 / Z_PARTS)

        chains = [[spawn(along(n, m)) for n in range(2)] for m in range(Z_PARTS)]
        b_done[h] = [spawn(arrive(c)) for c in range(2)]
        yield b_done[h] if C_PARTS == 1 else []

    def rotate(h, owner, first, size):
        work(0.05 + 0.15 * size / ROWS)
        r_acc[:, LANES[h]] += lax.dot_general(
            ql_all[owner].reshape(ROWS, ROWS)[first : first + size],
            t_all[h, owner, pl.ds(first, size)],
            (((0,), (0,)), ((), ())), preferred_element_type=f32,
        )

    def gather_rotate(h):
        r_acc[:, LANES[h]] = jnp.zeros((ROWS, HALF), f32)
        size = ROWS // C_PARTS
        waiting = []

        def put(owner, first, size):
            if left_task.done:
                rotate(h, owner, first, size)
            else:
                waiting.append((owner, first, size))

        def part(m):
            if C_PARTS == 2:
                yield [b_done[h][m]]

            def arrived(owner, n):
                if n is None:
                    put(owner, m * size, size)
                else:
                    put(owner, m * size + n * (size // 2), size // 2)

            yield gather_row(
                lambda owner: t_all.at[h, owner, pl.ds(m * size, size)],
                lambda owner, n: t_all.at[
                    h, owner, pl.ds(m * size + n * (size // 2), size // 2)
                ],
                arrived,
                False,
                "t", h, m,
            )

        tasks = [spawn(part(m)) for m in range(C_PARTS)]
        yield [left_task]
        for item in waiting:
            rotate(h, *item)
        waiting.clear()
        yield tasks

    def sum_row(h):
        rotated = r_acc[:, LANES[h]]
        out_copies.append(move(r_acc.at[:, LANES[h]], rotated_out.at[:, LANES[h]]))
        first, second = new_moments(first_old[:, LANES[h]], second_old[:, LANES[h]], rotated)
        step_all[:, LANES[h]] = (
            first / correct_first / (jnp.sqrt(second / correct_second) + epsilon)
        ).astype(bf16)
        work(0.3)

        size = ROWS // D_PARTS

        def back(owner, m):
            work(0.25 / D_PARTS)
            return jnp.dot(
                ql_all[owner].reshape(ROWS, ROWS)[m * size : (m + 1) * size],
                step_all[:, LANES[h]],
                preferred_element_type=f32,
            )

        def came(slot, rows):
            return b_recv[h, slot, rows].astype(f32)

        def own(slot, rows):
            return b_part[h, slot, rows]

        def go(slot, target, rows, m):
            return send(
                b_send.at[h, slot, rows], b_recv.at[h, slot, rows], target,
                "b", h, m, slot,
            )

        spans = [pl.ds(m * size, size) for m in range(D_PARTS)]
        opposite, side = [], []
        for m in range(D_PARTS):
            b_send[h, 0, spans[m]] = back(row_at(1, 2), m).astype(bf16)
            opposite.append(go(0, to_x, spans[m], m))
        for m in range(D_PARTS):
            side.append([])
            for n, s in enumerate(SIGNS):
                b_send[h, 1 + n, spans[m]] = back(row_at(1, s), m).astype(bf16)
                side[m].append(go(1 + n, to_y[s], spans[m], m))
        owners = (row_at(0, 2), row_at(0, 1), row_at(0, -1), row_at(1, 0), row)
        for slot, owner in enumerate(owners):
            for m in range(D_PARTS):
                b_part[h, slot, spans[m]] = back(owner, m)

        def reduce(m):
            last, after = [], []
            pieces = [pl.ds(m * size + n * (size // 2), size // 2) for n in range(2)]

            def across():
                yield [opposite[m]]
                total = own(0, spans[m]) + came(0, spans[m])
                b_send[h, 3, spans[m]] = total.astype(bf16)
                work(0.1)
                turned = [go(3, to_y[-s], pieces[n], m) for n, s in enumerate(SIGNS)]
                for n, s in enumerate(SIGNS):
                    after.append(spawn(along(n, s, turned[1 - n])))

            def along(n, s, move):
                yield [move]
                rows, rest = pieces[1 - n], pieces[n]
                total = own(1 + n, rows) + came(3, rows)
                b_send[h, 5 + n, rows] = total.astype(bf16)
                b_send[h, 5 + n, rest] = own(1 + n, rest).astype(bf16)
                work(0.1)
                last.append(go(5 + n, to_y[s], spans[m], m))

            def beside():
                yield side[m]
                total = own(3, spans[m]) + came(1, spans[m]) + came(2, spans[m])
                b_send[h, 4, spans[m]] = total.astype(bf16)
                work(0.1)
                last.append(go(4, to_x, spans[m], m))

            yield [spawn(across()), spawn(beside())]
            yield after
            yield last
            total = own(4, spans[m])
            for slot in (4, 5, 6):
                total = total + came(slot, spans[m])
            b_all[h, z, spans[m]] = total.astype(bf16)
            work(0.1)

        d_done[h] = [spawn(reduce(m)) for m in range(D_PARTS)]
        yield d_done[h] if D_PARTS == 1 else []

    def direction_part(owner, rows):
        work(0.4 if rows is ALL else 0.2)
        left = jnp.concatenate([b_all[h, owner, rows] for h in range(2)], axis=1)
        right = jnp.concatenate(
            [qr_all[h, owner].reshape(4 * COLS, HALF) for h in range(2)], axis=1
        )
        return lax.dot_general(
            left, right, (((1,), (1,)), ((), ())), preferred_element_type=f32
        )

    b_done, d_done = {}, {}
    seen = set()
    final = {}

    def add_direction(owner, what):
        if what in seen:
            if what == 0:
                d_acc[...] = direction_part(owner, ALL)
                seen.add("own")
            else:
                assert "own" in seen
                d_acc[...] += direction_part(owner, ALL)
        seen.add(what)

    def gather_z(h):
        count = {}

        def come(owner, what):
            count[what] = count.get(what, 0) + 1
            if count[what] == Z_PARTS:
                add_direction(owner, what)

        def along(n, m):
            if D_PARTS == 2:
                yield [d_done[h][m * 2 // Z_PARTS]]
            s = SIGNS[n]
            if n == 0:
                come(z, 0)
            view = b_all.at[h, z, ZPARTS[m]]
            move = same(view, to_z[s], "e", h, m, 0)
            for stage in (1, 2, 3):
                yield [move]
                owner = z_at(-s * stage)
                if stage < 3 or far_part(n, m):
                    view = b_all.at[h, owner, ZPARTS[m]]
                    move = same(view, to_z[s], "e", h, m, stage)
                come(owner, (n, stage))
            if far_part(n, m):
                final[h, m] = move

        yield [spawn(along(n, m)) for m in range(Z_PARTS) for n in range(2)]

    def pipeline(h):
        yield [right_tasks[h], grad_task]
        for part in (sum_z, gather_rotate, sum_row, gather_z):
            yield [spawn(part(h))]

    def finish(a):
        rows = PARTS[a]
        yield pipelines
        yield [final[h, m] for h in range(2) for m in range(Z_PARTS) if m * 2 // Z_PARTS == a]
        d_acc[rows] += direction_part(z_at(4), rows)
        for m in range(2):
            d_send[m, rows] = d_acc[rows, block(2 * m + (1 - k))].astype(bf16)
        core = send(d_send.at[pl.ds(0, 2), rows], d_recv.at[pl.ds(0, 2), rows], to_core)
        yield [core]
        total = d_acc[rows, block(u_far)] + d_recv[1 - xh, rows].astype(f32)
        d_send[2, rows] = total.astype(bf16)
        far_copy = send(d_send.at[2, rows], d_recv.at[2, rows], to_far)
        yield [far_copy]
        total = d_acc[rows, block(u)] + d_recv[xh, rows].astype(f32)
        d_out[rows] = total + d_recv[2, rows].astype(f32)
        out_copies.append(move(d_out.at[rows], direction_out.at[rows]))

    out_copies = []
    left_task = spawn(gather_left())
    right_tasks = [spawn(gather_right(h)) for h in range(2)]
    grad_task = spawn(gather_grad())
    pipelines = [spawn(pipeline(h)) for h in range(2)]
    for a in range(2):
        spawn(finish(a))
    order.run()
    for copy in order.started:
        copy.wait_send()
    for copy in out_copies:
        copy.wait()


def on_device(weight, grad, moment_first, moment_second, basis_left, basis_right):
    block = (ROWS, COLS)
    half = (ROWS, HALF)
    anywhere = pl.BlockSpec(memory_space=pl.ANY)
    rotated, direction = pl.pallas_call(
        kernel,
        name="soap_step",
        out_shape=(jax.ShapeDtypeStruct(block, f32), jax.ShapeDtypeStruct(block, f32)),
        in_specs=[anywhere] * 5,
        out_specs=(anywhere,) * 2,
        scratch_shapes=[
            pltpu.VMEM(block, f32),
            pltpu.VMEM(block, f32),
            pltpu.VMEM((2, 8, 4, COLS, HALF), bf16),
            pltpu.VMEM((ROWS, 4 * COLS), bf16),
            pltpu.VMEM((8, 2, 2, 128, ROWS), bf16),
            pltpu.VMEM((2, 8) + half, bf16),
            pltpu.VMEM(block, f32),
            pltpu.VMEM(block, bf16),
            pltpu.VMEM((2, 2, 4) + half, f32),
            pltpu.VMEM((2, 2, 4) + half, bf16),
            pltpu.VMEM((2, 2, 4) + half, bf16),
            pltpu.VMEM((2, 5) + half, f32),
            pltpu.VMEM((2, 7) + half, bf16),
            pltpu.VMEM((2, 7) + half, bf16),
            pltpu.VMEM((2, 8) + half, bf16),
            pltpu.VMEM((ROWS, 4 * COLS), f32),
            pltpu.VMEM(block, f32),
            pltpu.VMEM((3,) + block, bf16),
            pltpu.VMEM((3,) + block, bf16),
            pltpu.SemaphoreType.DMA((N_MSG,)),
            pltpu.SemaphoreType.DMA((N_MSG,)),
            pltpu.SemaphoreType.DMA((16,)),
        ],
        compiler_params=pltpu.CompilerParams(
            collective_id=0, has_side_effects=True, vmem_limit_bytes=56 * 2**20
        ),
        cost_estimate=pl.CostEstimate(
            flops=6 * 2**30, bytes_accessed=4 * 2**20, transcendentals=0
        ),
    )(grad, moment_first, moment_second, basis_left, basis_right)
    first_new, second_new = new_moments(moment_first, moment_second, rotated)
    update = direction.astype(bf16)
    wide = weight.astype(f32)
    new_weight = (wide - learn_rate * (direction + decay_rate * wide)).astype(bf16)
    return new_weight, update, first_new, second_new


def solution(mesh):
    spec = P("row", "col")
    turned = P("col", "row")
    return jax.shard_map(
        on_device,
        mesh=mesh,
        in_specs=(spec, spec, spec, spec, turned, turned),
        out_specs=(spec,) * 4,
        check_vma=False,
    )
```

```python
import jax
import jax.numpy as jnp
from jax import lax
from jax.experimental import pallas as pl
from jax.experimental.pallas import tpu as pltpu
from jax.sharding import PartitionSpec as P

beta_first = 0.9
beta_second = 0.95
correct_first = 1.0 - 0.9**10
correct_second = 1.0 - 0.95**10
epsilon = 1e-08
learn_rate = 0.001
decay_rate = 0.1

ROWS = 512
COLS = 256
HALF = 128
CUT = ROWS // 2
N_MSG = 300
SIGNS = (1, -1)
LANES = (pl.ds(0, HALF), pl.ds(HALF, HALF))
PARTS = (pl.ds(0, CUT), pl.ds(CUT, CUT))
ALL = pl.ds(0, ROWS)

f32 = jnp.float32
bf16 = jnp.bfloat16

RATE = {"core": 2.0e-6, "far": 18.5e-6, "x": 18.5e-6, "o": 18.5e-6, "y": 18.5e-6, "z": 18.5e-6}
RANK = {
    ("b", 0, 0, 0): 0.16, ("b", 0, 0, 1): 0.93, ("b", 0, 0, 2): 1.48, ("b", 0, 0, 3): 2.17,
    ("b", 0, 0, 4): 1.07, ("b", 0, 0, 5): 1.0, ("b", 0, 0, 6): 1.04, ("b", 0, 1, 0): 2.33,
    ("b", 0, 1, 1): -0.5, ("b", 0, 1, 2): 1.53, ("b", 0, 1, 3): 1.48, ("b", 0, 1, 4): 1.35,
    ("b", 0, 1, 5): 2.68, ("b", 0, 1, 6): 1.36, ("b", 1, 0, 0): 0.3, ("b", 1, 0, 1): 1.66,
    ("b", 1, 0, 2): 1.59, ("b", 1, 0, 3): 1.21, ("b", 1, 0, 4): -0.0, ("b", 1, 0, 5): 1.63,
    ("b", 1, 0, 6): -0.48, ("b", 1, 1, 0): -1.89, ("b", 1, 1, 1): 1.22, ("b", 1, 1, 2): -0.16,
    ("b", 1, 1, 3): 0.54, ("b", 1, 1, 4): 0.39, ("b", 1, 1, 5): 1.61, ("b", 1, 1, 6): 1.79,
    ("e", 0, 0, 0): 2.95, ("e", 0, 0, 1): 0.98, ("e", 0, 0, 2): 1.99, ("e", 0, 0, 3): 1.57,
    ("e", 0, 1, 0): 1.39, ("e", 0, 1, 1): 1.96, ("e", 0, 1, 2): 0.88, ("e", 0, 1, 3): 3.59,
    ("e", 1, 0, 0): 3.2, ("e", 1, 0, 1): 1.22, ("e", 1, 0, 2): 0.57, ("e", 1, 0, 3): 0.96,
    ("e", 1, 1, 0): 1.95, ("e", 1, 1, 1): 0.23, ("e", 1, 1, 2): 2.34, ("e", 1, 1, 3): 1.45,
    ("g", 0): 0.31, ("g", 1): 0.04, ("in", 0, 1): -1.84, ("in", 0, 2): -1.68, ("in", 0, 3): -1.3,
    ("in", 1, 1): 1.12, ("in", 1, 2): 1.75, ("in", 1, 3): -0.17, ("p", 0, False, 0): -0.1,
    ("p", 0, False, 1): 0.94, ("p", 0, False, 2): 1.27, ("p", 0, True, 0): 1.1,
    ("p", 0, True, 1): 0.11, ("p", 0, True, 2): 1.43, ("p", 0, True, 3): 0.42,
    ("p", 1, False, 0): 1.6, ("p", 1, False, 1): 1.53, ("p", 1, False, 2): 0.54,
    ("p", 1, True, 0): 0.04, ("p", 1, True, 1): 1.35, ("p", 1, True, 2): 1.73,
    ("p", 1, True, 3): -0.26, ("ql", "far"): -0.91, ("ql", 0, 0): 1.68, ("ql", 0, 1): 0.28,
    ("ql", 0, 2): 0.47, ("ql", 0, 3): 1.43, ("ql", 1, 0): 1.39, ("ql", 1, 1): 0.45,
    ("ql", 1, 2): 2.27, ("ql", 1, 3): 1.52, ("qr", 0, 0, "half"): 0.14,
    ("qr", 0, 0, "last"): 0.19, ("qr", 0, 0, "other"): -0.92, ("qr", 0, 0, "x"): -1.36,
    ("qr", 0, 0, "y"): -1.46, ("qr", 0, 1, "half"): -1.37, ("qr", 0, 1, "last"): -0.46,
    ("qr", 0, 1, "other"): 0.08, ("qr", 0, 1, "x"): -0.55, ("qr", 0, 1, "y"): 0.7,
    ("qr", 0, 2, "half"): -0.46, ("qr", 0, 2, "last"): -0.69, ("qr", 0, 2, "other"): -0.25,
    ("qr", 0, 2, "x"): -1.36, ("qr", 0, 2, "y"): -0.99, ("qr", 0, 3, "half"): 0.51,
    ("qr", 0, 3, "last"): -0.35, ("qr", 0, 3, "other"): -0.38, ("qr", 0, 3, "x"): -1.78,
    ("qr", 0, 3, "y"): -0.58, ("qr", 1, 0, "half"): 1.46, ("qr", 1, 0, "last"): 0.35,
    ("qr", 1, 0, "other"): 0.42, ("qr", 1, 0, "x"): 9.33, ("qr", 1, 0, "y"): 1.0,
    ("qr", 1, 1, "half"): 1.75, ("qr", 1, 1, "last"): 2.85, ("qr", 1, 1, "other"): 0.94,
    ("qr", 1, 1, "x"): 4.18, ("qr", 1, 1, "y"): 4.08, ("qr", 1, 2, "half"): 1.21,
    ("qr", 1, 2, "last"): 2.01, ("qr", 1, 2, "other"): 2.5, ("qr", 1, 2, "x"): 0.99,
    ("qr", 1, 2, "y"): 10.26, ("qr", 1, 3, "half"): -0.13, ("qr", 1, 3, "last"): 6.48,
    ("qr", 1, 3, "other"): 0.56, ("qr", 1, 3, "x"): 8.86, ("qr", 1, 3, "y"): 29.39,
    ("t", 0, 0, "half"): -1.46, ("t", 0, 0, "last"): -0.78, ("t", 0, 0, "other"): 1.41,
    ("t", 0, 0, "x"): 0.88, ("t", 0, 0, "y"): -1.57, ("t", 0, 1, "half"): 0.62,
    ("t", 0, 1, "last"): 0.23, ("t", 0, 1, "other"): -2.39, ("t", 0, 1, "x"): 1.15,
    ("t", 0, 1, "y"): -0.93, ("t", 1, 0, "half"): 0.91, ("t", 1, 0, "last"): 1.81,
    ("t", 1, 0, "other"): 1.45, ("t", 1, 0, "x"): 1.43, ("t", 1, 0, "y"): 1.3,
    ("t", 1, 1, "half"): -0.21, ("t", 1, 1, "last"): 1.2, ("t", 1, 1, "other"): 2.4,
    ("t", 1, 1, "x"): 1.58, ("t", 1, 1, "y"): 1.65,
}


def rank_of(*key):
    if key in RANK:
        return RANK[key]
    if key[0] in ("ql", "g"):
        return 0.45
    return float(key[1])


LAST_Y = {("qr", 0, 0), ("qr", 0, 3), ("qr", 1, 0), ("qr", 1, 2), ("qr", 1, 3), ("t", 0, 0)}
C_PARTS, D_PARTS = 2, 2
Z_PARTS = 2
ZPARTS = [pl.ds(m * (ROWS // Z_PARTS), ROWS // Z_PARTS) for m in range(Z_PARTS)]
AHEAD = 0.7
DELAY = {"core": 1.0, "far": 3.7, "x": 2.2, "o": 2.2, "y": 2.8, "z": 2.8}


def new_moments(first, second, rotated):
    return (
        beta_first * first + (1.0 - beta_first) * rotated,
        beta_second * second + (1.0 - beta_second) * rotated * rotated,
    )


class Moving:
    def __init__(self, copy):
        self.copy, self.arrival, self.here = copy, None, False

    def wait(self):
        if not self.here:
            self.copy.wait_recv()
        self.here = True


class Task:
    def __init__(self, steps):
        self.steps, self.waits, self.done = steps, (), False


class Order:
    def __init__(self, send_sem, recv_sem):
        self.send_sem, self.recv_sem = send_sem, recv_sem
        self.now, self.free, self.queues = 0.0, {}, {}
        self.count, self.started, self.tasks = 0, [], []

    def send(self, src, dst, target, *key):
        to, link, side = target
        rank = rank_of(*key) if key else 0.0
        n = self.count
        self.count += 1
        copy = pltpu.make_async_remote_copy(
            src_ref=src, dst_ref=dst, send_sem=self.send_sem.at[n],
            recv_sem=self.recv_sem.at[n], device_id=to, device_id_type=pl.DeviceIdType.MESH,
        )
        size = 2
        for extent in dst.shape:
            size *= extent
        move = Moving(copy)
        key = ("x" if link == "far" else link, side)
        queue = self.queues.setdefault(key, [])
        queue.append((rank, n, link, size, move))
        if link == "core":
            self.issue(key)
        return move

    def issue(self, key):
        queue = self.queues[key]
        entry = min(queue, key=lambda item: item[:2])
        queue.remove(entry)
        link, size, move = entry[2:]
        move.copy.start()
        self.now += 0.05
        self.started.append(move.copy)
        self.free[key] = max(self.now, self.free.get(key, 0.0)) + size * RATE[link]
        move.arrival = self.free[key] + DELAY[link]

    def work(self, us):
        self.now += us

    def pause(self):
        move = Moving(None)
        move.arrival, move.here = self.now, True
        return move

    def later(self, function, *tasks):
        def steps():
            yield [self.pause()] + list(tasks)
            function()

        return self.spawn(steps())

    def spawn(self, steps):
        task = Task(steps)
        self.tasks.append(task)
        self.step(task)
        return task

    def step(self, task):
        try:
            task.waits = next(task.steps)
        except StopIteration:
            task.done = True
            self.tasks.remove(task)

    def ready(self, task):
        time = 0.0
        for item in task.waits:
            if isinstance(item, Task):
                if not item.done:
                    return None
            elif item.arrival is None:
                return None
            else:
                time = max(time, item.arrival)
        return time

    def run(self):
        while self.tasks:
            events = []
            for n, task in enumerate(self.tasks):
                time = self.ready(task)
                if time is not None:
                    events.append((max(time, self.now), 1, time, n, task))
            for key, queue in self.queues.items():
                if queue:
                    time = max(self.now, self.free.get(key, 0.0) - AHEAD)
                    events.append((time, 0, 0.0, key, None))
            self.now, _, _, key, task = min(events, key=lambda event: event[:3])
            if task is None:
                self.issue(key)
                continue
            for item in task.waits:
                if isinstance(item, Moving):
                    item.wait()
            self.step(task)


def far_part(n, m):
    return m * 2 // Z_PARTS == n


def kernel(
    grad, moment_first, moment_second, ql, qr, rotated_out, direction_out,
    first_old, second_old, qr_all, g_all, ql_all, t_all, r_acc, step_all, p_part, p_send, p_recv,
    b_part, b_send, b_recv, b_all, d_acc, d_out, d_send, d_recv,
    send_sem, recv_sem, local_sem,
):
    row, col = lax.axis_index("row"), lax.axis_index("col")
    xl, y = lax.div(row, 4), lax.rem(row, 4)
    z, u = lax.div(col, 4), lax.rem(col, 4)
    xh, k = lax.div(u, 2), lax.rem(u, 2)

    def ring(value, shift, size):
        return lax.rem(value + (shift + size), size)

    def z_at(shift):
        return ring(z, shift, 8)

    def row_at(side, shift):
        return (xl if side == 0 else 1 - xl) * 4 + ring(y, shift, 4)

    u_core = xh * 2 + (1 - k)
    u_far = (1 - xh) * 2 + k
    u_cross = (1 - xh) * 2 + (1 - k)
    to_core = ((row, z * 4 + u_core), "core", 0)
    to_far = ((row, z * 4 + u_far), "far", 0)
    to_x = ((row_at(1, 0), col), "x", 0)
    to_other = ((row_at(1, 0), z * 4 + u_far), "o", 0)
    to_cross = ((row_at(1, 0), z * 4 + u_cross), "o", 0)
    to_y = {s: ((row_at(0, s), col), "y", s) for s in SIGNS}
    to_z = {s: ((row, z_at(s) * 4 + u), "z", s) for s in SIGNS}

    def block(index, h=None):
        if h is None:
            return pl.ds(pl.multiple_of(index * COLS, COLS), COLS)
        return pl.ds(pl.multiple_of(index * COLS + h * HALF, HALF), HALF)

    barrier = pltpu.get_barrier_semaphore()
    partners = (to_core, to_far, to_other, to_cross, to_z[1], to_z[-1], to_y[1], to_y[-1], to_x)
    for partner in partners:
        pl.semaphore_signal(
            barrier, inc=1, device_id=partner[0], device_id_type=pl.DeviceIdType.MESH
        )
    local = []

    def move(src, dst):
        copy = pltpu.make_async_copy(src, dst, local_sem.at[len(local)])
        copy.start()
        local.append(copy)
        return copy

    own_copies = [move(qr.at[:, block(u, h)], qr_all.at[h, row, u]) for h in range(2)]
    own_copies.append(move(ql, ql_all.at[z, xh, k]))
    own_copies.append(move(grad, g_all.at[:, block(u)]))
    old_copies = [move(moment_first, first_old), move(moment_second, second_old)]
    pl.semaphore_wait(barrier, len(partners))

    order = Order(send_sem, recv_sem)
    send, spawn, work, later = order.send, order.spawn, order.work, order.later

    def same(view, target, *key):
        return send(view, view, target, *key)

    def gather_row(full, half, arrived, flip, *key):
        last_y = key in LAST_Y

        def at(side, shift):
            return row_at(side if not flip else 1 - side, shift)

        view = full(at(0, 0))
        to_side = same(view, to_x, *key, "x")
        first = [same(view, to_y[s], *key, "y") for s in SIGNS]
        arrived(at(0, 0), None)

        def side():
            yield [to_side]
            other = at(1, 0)
            view = full(other)
            copies = [same(view, to_y[s], *key, "other") for s in SIGNS]
            arrived(other, None)
            for n, (copy, s) in enumerate(zip(copies, SIGNS)):
                yield [copy]
                arrived(at(1, -s), None)
                if last_y:
                    copies.append(same(half(at(1, -s), n), to_y[s], *key, "last"))
            for n, copy in enumerate(copies[2:]):
                yield [copy]
                arrived(at(1, 2), n)

        def along(n, s):
            yield [first[n]]
            view = half(at(0, -s), n)
            copy = same(view, to_y[s], *key, "half")
            arrived(at(0, -s), None)
            yield [copy]
            if not last_y:
                view = half(at(0, 2), n)
                copy = same(view, to_x, *key, "last")
            arrived(at(0, 2), n)
            if not last_y:
                yield [copy]
                arrived(at(1, 2), n)

        tasks = [spawn(along(n, s)) for n, s in enumerate(SIGNS)]
        return [spawn(side())] + tasks

    blocks = (u, u_core, u_far, u_cross)

    def qr_block(h, i):
        if i > 0:
            yield [qr_in[h, i]]
        source = blocks[i]
        yield gather_row(
            lambda owner: qr_all.at[h, owner, source, :],
            lambda owner, n: qr_all.at[h, owner, source, pl.ds(n * HALF, HALF)],
            lambda owner, n: None,
            i > 1,
            "qr", h, i,
        )

    qr_in = {}
    for h in range(2):
        for i, target in ((1, to_core), (2, to_other), (3, to_cross)):
            qr_in[h, i] = send(
                qr.at[:, block(blocks[i], h)], qr_all.at[h, row, u, :], target,
                "in", h, i,
            )
    ql_far = send(ql, ql_all.at[z, xh, k], to_far, "ql", "far")
    g_far = [
        send(grad.at[rows], g_all.at[rows, block(u)], to_far, "g", n)
        for n, rows in enumerate(PARTS)
    ]
    ql_core = send(ql, ql_all.at[z, xh, k], to_core)
    g_core = send(grad, g_all.at[:, block(u)], to_core)
    for copy in own_copies:
        copy.wait()

    def gather_right(h):
        yield [spawn(qr_block(h, i)) for i in range(4)]

    def gather_grad():
        g_cross = []
        for copy, rows in zip(g_far, PARTS):
            yield [copy]
            g_cross.append(same(g_all.at[rows, block(u_far)], to_core))
        yield [g_core] + g_cross

    ql_copies = [ql_core]

    def ql_chain(which):
        block_of = xh if which == 0 else 1 - xh
        if which == 1:
            yield [ql_far]
            ql_copies.append(same(ql_all.at[z, block_of, k], to_core))

        def along(n, s):
            move = same(ql_all.at[z, block_of, k], to_z[s], "ql", which, 0)
            for step in (1, 2, 3, 4):
                if step == 4 and n != which:
                    break
                yield [move]
                view = ql_all.at[z_at(-s * step), block_of, k]
                if step < 3 or (step == 3 and n == which):
                    move = same(view, to_z[s], "ql", which, step)
                ql_copies.append(same(view, to_core))

        yield [spawn(along(n, s)) for n, s in enumerate(SIGNS)]

    def gather_left():
        yield [spawn(ql_chain(which)) for which in range(2)]
        yield ql_copies

    def right_part(owner, h):
        work(0.3)
        return jnp.dot(
            g_all[...], qr_all[h, owner, :, :].reshape(4 * COLS, HALF),
            preferred_element_type=f32,
        )

    def sum_z(h):
        sends = {}

        def go(n, m, stage):
            return send(
                p_send.at[h, n, stage, ZPARTS[m]],
                p_recv.at[h, n, stage, ZPARTS[m]],
                to_z[SIGNS[n]],
                "p", h, far_part(n, m), stage,
            )

        term = right_part(z_at(4), h).astype(bf16)
        p_send[h, 0, 3, PARTS[0]] = term[:CUT]
        p_send[h, 1, 3, PARTS[1]] = term[CUT:]
        for m in range(Z_PARTS):
            n = 0 if far_part(0, m) else 1
            sends[n, m] = go(n, m, 3)
        for n, s in enumerate(SIGNS):
            term = right_part(z_at(3 * s), h)
            p_part[h, n, 3, :] = term
            p_send[h, n, 2, PARTS[1 - n]] = term[(1 - n) * CUT : (2 - n) * CUT].astype(bf16)
            for m in range(Z_PARTS):
                if not far_part(n, m):
                    sends[n, m] = go(n, m, 2)

        def compute(n, stage):
            def run():
                p_part[h, n, stage] = right_part(z_at(SIGNS[n] * stage), h)

            return later(run)

        computed = {(n, stage): compute(n, stage) for stage in (2, 1) for n in range(2)}
        computed[0, 0] = compute(0, 0)
        last = {}

        def along(n, m):
            move = sends[n, m]
            for stage in (3, 2, 1) if far_part(n, m) else (2, 1):
                yield [move] if stage == 3 else [move, computed[n, stage]]
                total = p_part[h, n, stage, ZPARTS[m]]
                total = total + p_recv[h, n, stage, ZPARTS[m]].astype(f32)
                p_send[h, n, stage - 1, ZPARTS[m]] = total.astype(bf16)
                work(0.2 / Z_PARTS)
                move = go(n, m, stage - 1)
            last[n, m] = move

        def arrive(c):
            parts = range(c * Z_PARTS // 2, (c + 1) * Z_PARTS // 2)
            for m in parts:
                yield chains[m]
                yield [last[n, m] for n in range(2)] + [computed[0, 0]]
                total = p_part[h, 0, 0, ZPARTS[m]]
                for n in range(2):
                    total = total + p_recv[h, n, 0, ZPARTS[m]].astype(f32)
                t_all[h, row, ZPARTS[m]] = total.astype(bf16)
                work(0.2 / Z_PARTS)

        chains = [[spawn(along(n, m)) for n in range(2)] for m in range(Z_PARTS)]
        b_done[h] = [spawn(arrive(c)) for c in range(2)]
        yield b_done[h] if C_PARTS == 1 else []

    def rotate(h, owner, first, size):
        work(0.05 + 0.15 * size / ROWS)
        r_acc[:, LANES[h]] += lax.dot_general(
            ql_all[owner].reshape(ROWS, ROWS)[first : first + size],
            t_all[h, owner, pl.ds(first, size)],
            (((0,), (0,)), ((), ())), preferred_element_type=f32,
        )

    def gather_rotate(h):
        r_acc[:, LANES[h]] = jnp.zeros((ROWS, HALF), f32)
        size = ROWS // C_PARTS
        waiting = []

        def put(owner, first, size):
            if left_task.done:
                rotate(h, owner, first, size)
            else:
                waiting.append((owner, first, size))

        def part(m):
            if C_PARTS == 2:
                yield [b_done[h][m]]

            def arrived(owner, n):
                if n is None:
                    put(owner, m * size, size)
                else:
                    put(owner, m * size + n * (size // 2), size // 2)

            yield gather_row(
                lambda owner: t_all.at[h, owner, pl.ds(m * size, size)],
                lambda owner, n: t_all.at[
                    h, owner, pl.ds(m * size + n * (size // 2), size // 2)
                ],
                arrived,
                False,
                "t", h, m,
            )

        tasks = [spawn(part(m)) for m in range(C_PARTS)]
        yield [left_task]
        for item in waiting:
            rotate(h, *item)
        waiting.clear()
        yield tasks

    def sum_row(h):
        rotated = r_acc[:, LANES[h]]
        while old_copies:
            old_copies.pop().wait()
        out_copies.append(move(r_acc.at[:, LANES[h]], rotated_out.at[:, LANES[h]]))
        first, second = new_moments(first_old[:, LANES[h]], second_old[:, LANES[h]], rotated)
        step_all[:, LANES[h]] = (
            first / correct_first / (jnp.sqrt(second / correct_second) + epsilon)
        ).astype(bf16)
        work(0.3)

        size = ROWS // D_PARTS

        def back(owner, m):
            work(0.25 / D_PARTS)
            return jnp.dot(
                ql_all[owner].reshape(ROWS, ROWS)[m * size : (m + 1) * size],
                step_all[:, LANES[h]],
                preferred_element_type=f32,
            )

        def came(slot, rows):
            return b_recv[h, slot, rows].astype(f32)

        def own(slot, rows):
            return b_part[h, slot, rows]

        def go(slot, target, rows, m):
            return send(
                b_send.at[h, slot, rows], b_recv.at[h, slot, rows], target,
                "b", h, m, slot,
            )

        spans = [pl.ds(m * size, size) for m in range(D_PARTS)]
        opposite, side = [], []
        for m in range(D_PARTS):
            b_send[h, 0, spans[m]] = back(row_at(1, 2), m).astype(bf16)
            opposite.append(go(0, to_x, spans[m], m))
        for m in range(D_PARTS):
            side.append([])
            for n, s in enumerate(SIGNS):
                b_send[h, 1 + n, spans[m]] = back(row_at(1, s), m).astype(bf16)
                side[m].append(go(1 + n, to_y[s], spans[m], m))
        owners = (row_at(0, 2), row_at(0, 1), row_at(0, -1), row_at(1, 0), row)

        def compute(slot, m):
            def run():
                b_part[h, slot, spans[m]] = back(owners[slot], m)

            return later(run)

        computed = {(slot, m): compute(slot, m) for slot in range(5) for m in range(D_PARTS)}

        def reduce(m):
            last, after = [], []
            pieces = [pl.ds(m * size + n * (size // 2), size // 2) for n in range(2)]

            def across():
                yield [opposite[m], computed[0, m]]
                total = own(0, spans[m]) + came(0, spans[m])
                b_send[h, 3, spans[m]] = total.astype(bf16)
                work(0.1)
                turned = [go(3, to_y[-s], pieces[n], m) for n, s in enumerate(SIGNS)]
                for n, s in enumerate(SIGNS):
                    after.append(spawn(along(n, s, turned[1 - n])))

            def along(n, s, move):
                yield [move, computed[1 + n, m]]
                rows, rest = pieces[1 - n], pieces[n]
                total = own(1 + n, rows) + came(3, rows)
                b_send[h, 5 + n, rows] = total.astype(bf16)
                b_send[h, 5 + n, rest] = own(1 + n, rest).astype(bf16)
                work(0.1)
                last.append(go(5 + n, to_y[s], spans[m], m))

            def beside():
                yield side[m] + [computed[3, m]]
                total = own(3, spans[m]) + came(1, spans[m]) + came(2, spans[m])
                b_send[h, 4, spans[m]] = total.astype(bf16)
                work(0.1)
                last.append(go(4, to_x, spans[m], m))

            yield [spawn(across()), spawn(beside())]
            yield after
            yield last + [computed[4, m]]
            total = own(4, spans[m])
            for slot in (4, 5, 6):
                total = total + came(slot, spans[m])
            b_all[h, z, spans[m]] = total.astype(bf16)
            work(0.1)

        d_done[h] = [spawn(reduce(m)) for m in range(D_PARTS)]
        yield d_done[h] if D_PARTS == 1 else []

    def direction_part(owner, rows):
        work(0.4 if rows is ALL else 0.2)
        left = jnp.concatenate([b_all[h, owner, rows] for h in range(2)], axis=1)
        right = jnp.concatenate(
            [qr_all[h, owner].reshape(4 * COLS, HALF) for h in range(2)], axis=1
        )
        return lax.dot_general(
            left, right, (((1,), (1,)), ((), ())), preferred_element_type=f32
        )

    b_done, d_done = {}, {}
    seen, added = set(), []
    final = {}

    def add_direction(owner, what):
        def first():
            d_acc[...] = direction_part(owner, ALL)

        def add():
            d_acc[...] += direction_part(owner, ALL)

        if what in seen:
            if what == 0:
                added.append(later(first))
            else:
                added.append(later(add, added[0]))
        seen.add(what)

    def gather_z(h):
        count = {}

        def come(owner, what):
            count[what] = count.get(what, 0) + 1
            if count[what] == Z_PARTS:
                add_direction(owner, what)

        def along(n, m):
            if D_PARTS == 2:
                yield [d_done[h][m * 2 // Z_PARTS]]
            s = SIGNS[n]
            if n == 0:
                come(z, 0)
            view = b_all.at[h, z, ZPARTS[m]]
            move = same(view, to_z[s], "e", h, m, 0)
            for stage in (1, 2, 3):
                yield [move]
                owner = z_at(-s * stage)
                if stage < 3 or far_part(n, m):
                    view = b_all.at[h, owner, ZPARTS[m]]
                    move = same(view, to_z[s], "e", h, m, stage)
                come(owner, (n, stage))
            if far_part(n, m):
                final[h, m] = move

        yield [spawn(along(n, m)) for m in range(Z_PARTS) for n in range(2)]

    def pipeline(h):
        yield [right_tasks[h], grad_task]
        for part in (sum_z, gather_rotate, sum_row, gather_z):
            yield [spawn(part(h))]

    def finish(a):
        rows = PARTS[a]
        yield pipelines
        yield added
        yield [final[h, m] for h in range(2) for m in range(Z_PARTS) if m * 2 // Z_PARTS == a]
        d_acc[rows] += direction_part(z_at(4), rows)
        for m in range(2):
            d_send[m, rows] = d_acc[rows, block(2 * m + (1 - k))].astype(bf16)
        core = send(d_send.at[pl.ds(0, 2), rows], d_recv.at[pl.ds(0, 2), rows], to_core)
        yield [core]
        total = d_acc[rows, block(u_far)] + d_recv[1 - xh, rows].astype(f32)
        d_send[2, rows] = total.astype(bf16)
        far_copy = send(d_send.at[2, rows], d_recv.at[2, rows], to_far)
        yield [far_copy]
        total = d_acc[rows, block(u)] + d_recv[xh, rows].astype(f32)
        d_out[rows] = total + d_recv[2, rows].astype(f32)
        out_copies.append(move(d_out.at[rows], direction_out.at[rows]))

    out_copies = []
    left_task = spawn(gather_left())
    right_tasks = [spawn(gather_right(h)) for h in range(2)]
    grad_task = spawn(gather_grad())
    pipelines = [spawn(pipeline(h)) for h in range(2)]
    for a in range(2):
        spawn(finish(a))
    order.run()
    for copy in order.started:
        copy.wait_send()
    for copy in out_copies:
        copy.wait()


def on_device(weight, grad, moment_first, moment_second, basis_left, basis_right):
    block = (ROWS, COLS)
    half = (ROWS, HALF)
    anywhere = pl.BlockSpec(memory_space=pl.ANY)
    rotated, direction = pl.pallas_call(
        kernel,
        name="soap_step",
        out_shape=(jax.ShapeDtypeStruct(block, f32), jax.ShapeDtypeStruct(block, f32)),
        in_specs=[anywhere] * 5,
        out_specs=(anywhere,) * 2,
        scratch_shapes=[
            pltpu.VMEM(block, f32),
            pltpu.VMEM(block, f32),
            pltpu.VMEM((2, 8, 4, COLS, HALF), bf16),
            pltpu.VMEM((ROWS, 4 * COLS), bf16),
            pltpu.VMEM((8, 2, 2, 128, ROWS), bf16),
            pltpu.VMEM((2, 8) + half, bf16),
            pltpu.VMEM(block, f32),
            pltpu.VMEM(block, bf16),
            pltpu.VMEM((2, 2, 4) + half, f32),
            pltpu.VMEM((2, 2, 4) + half, bf16),
            pltpu.VMEM((2, 2, 4) + half, bf16),
            pltpu.VMEM((2, 5) + half, f32),
            pltpu.VMEM((2, 7) + half, bf16),
            pltpu.VMEM((2, 7) + half, bf16),
            pltpu.VMEM((2, 8) + half, bf16),
            pltpu.VMEM((ROWS, 4 * COLS), f32),
            pltpu.VMEM(block, f32),
            pltpu.VMEM((3,) + block, bf16),
            pltpu.VMEM((3,) + block, bf16),
            pltpu.SemaphoreType.DMA((N_MSG,)),
            pltpu.SemaphoreType.DMA((N_MSG,)),
            pltpu.SemaphoreType.DMA((16,)),
        ],
        compiler_params=pltpu.CompilerParams(
            collective_id=0, has_side_effects=True, vmem_limit_bytes=56 * 2**20
        ),
        cost_estimate=pl.CostEstimate(
            flops=6 * 2**30, bytes_accessed=4 * 2**20, transcendentals=0
        ),
    )(grad, moment_first, moment_second, basis_left, basis_right)
    first_new, second_new = new_moments(moment_first, moment_second, rotated)
    update = direction.astype(bf16)
    wide = weight.astype(f32)
    new_weight = (wide - learn_rate * (direction + decay_rate * wide)).astype(bf16)
    return new_weight, update, first_new, second_new


def solution(mesh):
    spec = P("row", "col")
    turned = P("col", "row")
    return jax.shard_map(
        on_device,
        mesh=mesh,
        in_specs=(spec, spec, spec, spec, turned, turned),
        out_specs=(spec,) * 4,
        check_vma=False,
    )
```

```python
import jax
import jax.numpy as jnp
from jax import lax
from jax.experimental import pallas as pl
from jax.experimental.pallas import tpu as pltpu
from jax.sharding import PartitionSpec as P

beta_first = 0.9
beta_second = 0.95
correct_first = 1.0 - 0.9**10
correct_second = 1.0 - 0.95**10
epsilon = 1e-08
learn_rate = 0.001
decay_rate = 0.1

ROWS = 512
COLS = 256
HALF = 128
CUT = ROWS // 2
N_MSG = 300
SIGNS = (1, -1)
LANES = (pl.ds(0, HALF), pl.ds(HALF, HALF))
PARTS = (pl.ds(0, CUT), pl.ds(CUT, CUT))
ALL = pl.ds(0, ROWS)

f32 = jnp.float32
bf16 = jnp.bfloat16

RATE = {"core": 2.0e-6, "far": 18.5e-6, "x": 18.5e-6, "o": 18.5e-6, "y": 18.5e-6, "z": 18.5e-6}
RANK = {
    ("b", 0, 0, 0): 0.16, ("b", 0, 0, 1): 0.93, ("b", 0, 0, 2): 1.48, ("b", 0, 0, 3): 2.17,
    ("b", 0, 0, 4): 1.07, ("b", 0, 0, 5): 1.0, ("b", 0, 0, 6): 1.04, ("b", 0, 1, 0): 2.33,
    ("b", 0, 1, 1): -0.5, ("b", 0, 1, 2): 1.53, ("b", 0, 1, 3): 1.48, ("b", 0, 1, 4): 1.35,
    ("b", 0, 1, 5): 2.68, ("b", 0, 1, 6): 1.36, ("b", 1, 0, 0): 0.3, ("b", 1, 0, 1): 1.66,
    ("b", 1, 0, 2): 1.59, ("b", 1, 0, 3): 1.21, ("b", 1, 0, 4): -0.0, ("b", 1, 0, 5): 1.63,
    ("b", 1, 0, 6): -0.48, ("b", 1, 1, 0): -1.89, ("b", 1, 1, 1): 1.22, ("b", 1, 1, 2): -0.16,
    ("b", 1, 1, 3): 0.54, ("b", 1, 1, 4): 0.39, ("b", 1, 1, 5): 1.61, ("b", 1, 1, 6): 1.79,
    ("e", 0, 0, 0): 2.95, ("e", 0, 0, 1): 0.98, ("e", 0, 0, 2): 1.99, ("e", 0, 0, 3): 1.57,
    ("e", 0, 1, 0): 1.39, ("e", 0, 1, 1): 1.96, ("e", 0, 1, 2): 0.88, ("e", 0, 1, 3): 3.59,
    ("e", 1, 0, 0): 3.2, ("e", 1, 0, 1): 1.22, ("e", 1, 0, 2): 0.57, ("e", 1, 0, 3): 0.96,
    ("e", 1, 1, 0): 1.95, ("e", 1, 1, 1): 0.23, ("e", 1, 1, 2): 2.34, ("e", 1, 1, 3): 1.45,
    ("g", 0): 0.31, ("g", 1): 0.04, ("in", 0, 1): -1.84, ("in", 0, 2): -1.68, ("in", 0, 3): -1.3,
    ("in", 1, 1): 1.12, ("in", 1, 2): 1.75, ("in", 1, 3): -0.17, ("p", 0, False, 0): -0.1,
    ("p", 0, False, 1): 0.94, ("p", 0, False, 2): 1.27, ("p", 0, True, 0): 1.1,
    ("p", 0, True, 1): 0.11, ("p", 0, True, 2): 1.43, ("p", 0, True, 3): 0.42,
    ("p", 1, False, 0): 1.6, ("p", 1, False, 1): 1.53, ("p", 1, False, 2): 0.54,
    ("p", 1, True, 0): 0.04, ("p", 1, True, 1): 1.35, ("p", 1, True, 2): 1.73,
    ("p", 1, True, 3): -0.26, ("ql", "far"): -0.91, ("ql", 0, 0): 1.68, ("ql", 0, 1): 0.28,
    ("ql", 0, 2): 0.47, ("ql", 0, 3): 1.43, ("ql", 1, 0): 1.39, ("ql", 1, 1): 0.45,
    ("ql", 1, 2): 2.27, ("ql", 1, 3): 1.52, ("qr", 0, 0, "half"): 0.14,
    ("qr", 0, 0, "last"): 0.19, ("qr", 0, 0, "other"): -0.92, ("qr", 0, 0, "x"): -1.36,
    ("qr", 0, 0, "y"): -1.46, ("qr", 0, 1, "half"): -1.37, ("qr", 0, 1, "last"): -0.46,
    ("qr", 0, 1, "other"): 0.08, ("qr", 0, 1, "x"): -0.55, ("qr", 0, 1, "y"): 0.7,
    ("qr", 0, 2, "half"): -0.46, ("qr", 0, 2, "last"): -0.69, ("qr", 0, 2, "other"): -0.25,
    ("qr", 0, 2, "x"): -1.36, ("qr", 0, 2, "y"): -0.99, ("qr", 0, 3, "half"): 0.51,
    ("qr", 0, 3, "last"): -0.35, ("qr", 0, 3, "other"): -0.38, ("qr", 0, 3, "x"): -1.78,
    ("qr", 0, 3, "y"): -0.58, ("qr", 1, 0, "half"): 1.46, ("qr", 1, 0, "last"): 0.35,
    ("qr", 1, 0, "other"): 0.42, ("qr", 1, 0, "x"): 9.33, ("qr", 1, 0, "y"): 1.0,
    ("qr", 1, 1, "half"): 1.75, ("qr", 1, 1, "last"): 2.85, ("qr", 1, 1, "other"): 0.94,
    ("qr", 1, 1, "x"): 4.18, ("qr", 1, 1, "y"): 4.08, ("qr", 1, 2, "half"): 1.21,
    ("qr", 1, 2, "last"): 2.01, ("qr", 1, 2, "other"): 2.5, ("qr", 1, 2, "x"): 0.99,
    ("qr", 1, 2, "y"): 10.26, ("qr", 1, 3, "half"): -0.13, ("qr", 1, 3, "last"): 6.48,
    ("qr", 1, 3, "other"): 0.56, ("qr", 1, 3, "x"): 8.86, ("qr", 1, 3, "y"): 29.39,
    ("t", 0, 0, "half"): -1.46, ("t", 0, 0, "last"): -0.78, ("t", 0, 0, "other"): 1.41,
    ("t", 0, 0, "x"): 0.88, ("t", 0, 0, "y"): -1.57, ("t", 0, 1, "half"): 0.62,
    ("t", 0, 1, "last"): 0.23, ("t", 0, 1, "other"): -2.39, ("t", 0, 1, "x"): 1.15,
    ("t", 0, 1, "y"): -0.93, ("t", 1, 0, "half"): 0.91, ("t", 1, 0, "last"): 1.81,
    ("t", 1, 0, "other"): 1.45, ("t", 1, 0, "x"): 1.43, ("t", 1, 0, "y"): 1.3,
    ("t", 1, 1, "half"): -0.21, ("t", 1, 1, "last"): 1.2, ("t", 1, 1, "other"): 2.4,
    ("t", 1, 1, "x"): 1.58, ("t", 1, 1, "y"): 1.65,
}


def rank_of(*key):
    if key in RANK:
        return RANK[key]
    if key[0] in ("ql", "g"):
        return 0.45
    return float(key[1])


LAST_Y = {("qr", 0, 0), ("qr", 0, 3), ("qr", 1, 0), ("qr", 1, 2), ("qr", 1, 3), ("t", 0, 0)}
C_PARTS, D_PARTS = 2, 2
Z_PARTS = 2
ZPARTS = [pl.ds(m * (ROWS // Z_PARTS), ROWS // Z_PARTS) for m in range(Z_PARTS)]
AHEAD = 0.9
DELAY = {"core": 1.0, "far": 3.7, "x": 2.2, "o": 2.2, "y": 2.8, "z": 2.8}


def new_moments(first, second, rotated):
    return (
        beta_first * first + (1.0 - beta_first) * rotated,
        beta_second * second + (1.0 - beta_second) * rotated * rotated,
    )


class Moving:
    def __init__(self, copy):
        self.copy, self.arrival, self.here = copy, None, False

    def wait(self):
        if not self.here:
            self.copy.wait_recv()
        self.here = True


class Task:
    def __init__(self, steps):
        self.steps, self.waits, self.done = steps, (), False


class Order:
    def __init__(self, send_sem, recv_sem):
        self.send_sem, self.recv_sem = send_sem, recv_sem
        self.now, self.free, self.queues = 0.0, {}, {}
        self.count, self.started, self.tasks = 0, [], []

    def send(self, src, dst, target, *key):
        to, link, side = target
        rank = rank_of(*key) if key else 0.0
        n = self.count
        self.count += 1
        copy = pltpu.make_async_remote_copy(
            src_ref=src, dst_ref=dst, send_sem=self.send_sem.at[n],
            recv_sem=self.recv_sem.at[n], device_id=to, device_id_type=pl.DeviceIdType.MESH,
        )
        size = 2
        for extent in dst.shape:
            size *= extent
        move = Moving(copy)
        key = ("x" if link == "far" else link, side)
        queue = self.queues.setdefault(key, [])
        queue.append((rank, n, link, size, move))
        if link == "core":
            self.issue(key)
        return move

    def issue(self, key):
        queue = self.queues[key]
        entry = min(queue, key=lambda item: item[:2])
        queue.remove(entry)
        link, size, move = entry[2:]
        move.copy.start()
        self.now += 0.05
        self.started.append(move.copy)
        self.free[key] = max(self.now, self.free.get(key, 0.0)) + size * RATE[link]
        move.arrival = self.free[key] + DELAY[link]

    def work(self, us):
        self.now += us

    def pause(self):
        move = Moving(None)
        move.arrival, move.here = self.now, True
        return move

    def later(self, function, *tasks):
        def steps():
            yield [self.pause()] + list(tasks)
            function()

        return self.spawn(steps())

    def spawn(self, steps):
        task = Task(steps)
        self.tasks.append(task)
        self.step(task)
        return task

    def step(self, task):
        try:
            task.waits = next(task.steps)
        except StopIteration:
            task.done = True
            self.tasks.remove(task)

    def ready(self, task):
        time = 0.0
        for item in task.waits:
            if isinstance(item, Task):
                if not item.done:
                    return None
            elif item.arrival is None:
                return None
            else:
                time = max(time, item.arrival)
        return time

    def run(self):
        while self.tasks:
            events = []
            for n, task in enumerate(self.tasks):
                time = self.ready(task)
                if time is not None:
                    events.append((max(time, self.now), 1, time, n, task))
            for key, queue in self.queues.items():
                if queue:
                    time = max(self.now, self.free.get(key, 0.0) - AHEAD)
                    events.append((time, 0, 0.0, key, None))
            self.now, _, _, key, task = min(events, key=lambda event: event[:3])
            if task is None:
                self.issue(key)
                continue
            for item in task.waits:
                if isinstance(item, Moving):
                    item.wait()
            self.step(task)


def far_part(n, m):
    return m * 2 // Z_PARTS == n


def kernel(
    grad, moment_first, moment_second, ql, qr, rotated_out, direction_out,
    first_old, second_old, qr_all, g_all, ql_all, t_all, r_acc, step_all, p_part, p_send, p_recv,
    b_part, b_send, b_recv, b_all, d_acc, d_out, d_send, d_recv,
    send_sem, recv_sem, local_sem,
):
    row, col = lax.axis_index("row"), lax.axis_index("col")
    xl, y = lax.div(row, 4), lax.rem(row, 4)
    z, u = lax.div(col, 4), lax.rem(col, 4)
    xh, k = lax.div(u, 2), lax.rem(u, 2)

    def ring(value, shift, size):
        return lax.rem(value + (shift + size), size)

    def z_at(shift):
        return ring(z, shift, 8)

    def row_at(side, shift):
        return (xl if side == 0 else 1 - xl) * 4 + ring(y, shift, 4)

    u_core = xh * 2 + (1 - k)
    u_far = (1 - xh) * 2 + k
    u_cross = (1 - xh) * 2 + (1 - k)
    to_core = ((row, z * 4 + u_core), "core", 0)
    to_far = ((row, z * 4 + u_far), "far", 0)
    to_x = ((row_at(1, 0), col), "x", 0)
    to_other = ((row_at(1, 0), z * 4 + u_far), "o", 0)
    to_cross = ((row_at(1, 0), z * 4 + u_cross), "o", 0)
    to_y = {s: ((row_at(0, s), col), "y", s) for s in SIGNS}
    to_z = {s: ((row, z_at(s) * 4 + u), "z", s) for s in SIGNS}

    def block(index, h=None):
        if h is None:
            return pl.ds(pl.multiple_of(index * COLS, COLS), COLS)
        return pl.ds(pl.multiple_of(index * COLS + h * HALF, HALF), HALF)

    barrier = pltpu.get_barrier_semaphore()
    partners = (to_core, to_far, to_other, to_cross, to_z[1], to_z[-1], to_y[1], to_y[-1], to_x)
    for partner in partners:
        pl.semaphore_signal(
            barrier, inc=1, device_id=partner[0], device_id_type=pl.DeviceIdType.MESH
        )
    local = []

    def move(src, dst):
        copy = pltpu.make_async_copy(src, dst, local_sem.at[len(local)])
        copy.start()
        local.append(copy)
        return copy

    own_copies = [move(qr.at[:, block(u, h)], qr_all.at[h, row, u]) for h in range(2)]
    own_copies.append(move(ql, ql_all.at[z, xh, k]))
    own_copies.append(move(grad, g_all.at[:, block(u)]))
    old_copies = [move(moment_first, first_old), move(moment_second, second_old)]
    pl.semaphore_wait(barrier, len(partners))

    order = Order(send_sem, recv_sem)
    send, spawn, work, later = order.send, order.spawn, order.work, order.later

    def same(view, target, *key):
        return send(view, view, target, *key)

    def gather_row(full, half, arrived, flip, *key):
        last_y = key in LAST_Y

        def at(side, shift):
            return row_at(side if not flip else 1 - side, shift)

        view = full(at(0, 0))
        to_side = same(view, to_x, *key, "x")
        first = [same(view, to_y[s], *key, "y") for s in SIGNS]
        arrived(at(0, 0), None)

        def side():
            yield [to_side]
            other = at(1, 0)
            view = full(other)
            copies = [same(view, to_y[s], *key, "other") for s in SIGNS]
            arrived(other, None)
            for n, (copy, s) in enumerate(zip(copies, SIGNS)):
                yield [copy]
                arrived(at(1, -s), None)
                if last_y:
                    copies.append(same(half(at(1, -s), n), to_y[s], *key, "last"))
            for n, copy in enumerate(copies[2:]):
                yield [copy]
                arrived(at(1, 2), n)

        def along(n, s):
            yield [first[n]]
            view = half(at(0, -s), n)
            copy = same(view, to_y[s], *key, "half")
            arrived(at(0, -s), None)
            yield [copy]
            if not last_y:
                view = half(at(0, 2), n)
                copy = same(view, to_x, *key, "last")
            arrived(at(0, 2), n)
            if not last_y:
                yield [copy]
                arrived(at(1, 2), n)

        tasks = [spawn(along(n, s)) for n, s in enumerate(SIGNS)]
        return [spawn(side())] + tasks

    blocks = (u, u_core, u_far, u_cross)

    def qr_block(h, i):
        if i > 0:
            yield [qr_in[h, i]]
        source = blocks[i]
        yield gather_row(
            lambda owner: qr_all.at[h, owner, source, :],
            lambda owner, n: qr_all.at[h, owner, source, pl.ds(n * HALF, HALF)],
            lambda owner, n: None,
            i > 1,
            "qr", h, i,
        )

    qr_in = {}
    for h in range(2):
        for i, target in ((1, to_core), (2, to_other), (3, to_cross)):
            qr_in[h, i] = send(
                qr.at[:, block(blocks[i], h)], qr_all.at[h, row, u, :], target,
                "in", h, i,
            )
    ql_far = send(ql, ql_all.at[z, xh, k], to_far, "ql", "far")
    g_far = [
        send(grad.at[rows], g_all.at[rows, block(u)], to_far, "g", n)
        for n, rows in enumerate(PARTS)
    ]
    ql_core = send(ql, ql_all.at[z, xh, k], to_core)
    g_core = send(grad, g_all.at[:, block(u)], to_core)
    for copy in own_copies:
        copy.wait()

    def gather_right(h):
        yield [spawn(qr_block(h, i)) for i in range(4)]

    def gather_grad():
        g_cross = []
        for copy, rows in zip(g_far, PARTS):
            yield [copy]
            g_cross.append(same(g_all.at[rows, block(u_far)], to_core))
        yield [g_core] + g_cross

    ql_copies = [ql_core]

    def ql_chain(which):
        block_of = xh if which == 0 else 1 - xh
        if which == 1:
            yield [ql_far]
            ql_copies.append(same(ql_all.at[z, block_of, k], to_core))

        def along(n, s):
            move = same(ql_all.at[z, block_of, k], to_z[s], "ql", which, 0)
            for step in (1, 2, 3, 4):
                if step == 4 and n != which:
                    break
                yield [move]
                view = ql_all.at[z_at(-s * step), block_of, k]
                if step < 3 or (step == 3 and n == which):
                    move = same(view, to_z[s], "ql", which, step)
                ql_copies.append(same(view, to_core))

        yield [spawn(along(n, s)) for n, s in enumerate(SIGNS)]

    def gather_left():
        yield [spawn(ql_chain(which)) for which in range(2)]
        yield ql_copies

    def right_part(owner, h):
        work(0.3)
        return jnp.dot(
            g_all[...], qr_all[h, owner, :, :].reshape(4 * COLS, HALF),
            preferred_element_type=f32,
        )

    def sum_z(h):
        sends = {}

        def go(n, m, stage):
            return send(
                p_send.at[h, n, stage, ZPARTS[m]],
                p_recv.at[h, n, stage, ZPARTS[m]],
                to_z[SIGNS[n]],
                "p", h, far_part(n, m), stage,
            )

        term = right_part(z_at(4), h).astype(bf16)
        p_send[h, 0, 3, PARTS[0]] = term[:CUT]
        p_send[h, 1, 3, PARTS[1]] = term[CUT:]
        for m in range(Z_PARTS):
            n = 0 if far_part(0, m) else 1
            sends[n, m] = go(n, m, 3)
        for n, s in enumerate(SIGNS):
            term = right_part(z_at(3 * s), h)
            p_part[h, n, 3, :] = term
            p_send[h, n, 2, PARTS[1 - n]] = term[(1 - n) * CUT : (2 - n) * CUT].astype(bf16)
            for m in range(Z_PARTS):
                if not far_part(n, m):
                    sends[n, m] = go(n, m, 2)

        def compute(n, stage):
            def run():
                p_part[h, n, stage] = right_part(z_at(SIGNS[n] * stage), h)

            return later(run)

        computed = {(n, stage): compute(n, stage) for stage in (2, 1) for n in range(2)}
        computed[0, 0] = compute(0, 0)
        last = {}

        def along(n, m):
            move = sends[n, m]
            for stage in (3, 2, 1) if far_part(n, m) else (2, 1):
                yield [move] if stage == 3 else [move, computed[n, stage]]
                total = p_part[h, n, stage, ZPARTS[m]]
                total = total + p_recv[h, n, stage, ZPARTS[m]].astype(f32)
                p_send[h, n, stage - 1, ZPARTS[m]] = total.astype(bf16)
                work(0.2 / Z_PARTS)
                move = go(n, m, stage - 1)
            last[n, m] = move

        def arrive(c):
            parts = range(c * Z_PARTS // 2, (c + 1) * Z_PARTS // 2)
            for m in parts:
                yield chains[m]
                yield [last[n, m] for n in range(2)] + [computed[0, 0]]
                total = p_part[h, 0, 0, ZPARTS[m]]
                for n in range(2):
                    total = total + p_recv[h, n, 0, ZPARTS[m]].astype(f32)
                t_all[h, row, ZPARTS[m]] = total.astype(bf16)
                work(0.2 / Z_PARTS)

        chains = [[spawn(along(n, m)) for n in range(2)] for m in range(Z_PARTS)]
        b_done[h] = [spawn(arrive(c)) for c in range(2)]
        yield b_done[h] if C_PARTS == 1 else []

    def rotate(h, owner, first, size):
        work(0.05 + 0.15 * size / ROWS)
        r_acc[:, LANES[h]] += lax.dot_general(
            ql_all[owner].reshape(ROWS, ROWS)[first : first + size],
            t_all[h, owner, pl.ds(first, size)],
            (((0,), (0,)), ((), ())), preferred_element_type=f32,
        )

    def gather_rotate(h):
        r_acc[:, LANES[h]] = jnp.zeros((ROWS, HALF), f32)
        size = ROWS // C_PARTS
        waiting = []

        def put(owner, first, size):
            if left_task.done:
                rotate(h, owner, first, size)
            else:
                waiting.append((owner, first, size))

        def part(m):
            if C_PARTS == 2:
                yield [b_done[h][m]]

            def arrived(owner, n):
                if n is None:
                    put(owner, m * size, size)
                else:
                    put(owner, m * size + n * (size // 2), size // 2)

            yield gather_row(
                lambda owner: t_all.at[h, owner, pl.ds(m * size, size)],
                lambda owner, n: t_all.at[
                    h, owner, pl.ds(m * size + n * (size // 2), size // 2)
                ],
                arrived,
                False,
                "t", h, m,
            )

        tasks = [spawn(part(m)) for m in range(C_PARTS)]
        yield [left_task]
        for item in waiting:
            rotate(h, *item)
        waiting.clear()
        yield tasks

    def sum_row(h):
        rotated = r_acc[:, LANES[h]]
        while old_copies:
            old_copies.pop().wait()
        out_copies.append(move(r_acc.at[:, LANES[h]], rotated_out.at[:, LANES[h]]))
        first, second = new_moments(first_old[:, LANES[h]], second_old[:, LANES[h]], rotated)
        step_all[:, LANES[h]] = (
            first / correct_first / (jnp.sqrt(second / correct_second) + epsilon)
        ).astype(bf16)
        work(0.3)

        size = ROWS // D_PARTS

        def back(owner, m):
            work(0.25 / D_PARTS)
            return jnp.dot(
                ql_all[owner].reshape(ROWS, ROWS)[m * size : (m + 1) * size],
                step_all[:, LANES[h]],
                preferred_element_type=f32,
            )

        def came(slot, rows):
            return b_recv[h, slot, rows].astype(f32)

        def own(slot, rows):
            return b_part[h, slot, rows]

        def go(slot, target, rows, m):
            return send(
                b_send.at[h, slot, rows], b_recv.at[h, slot, rows], target,
                "b", h, m, slot,
            )

        spans = [pl.ds(m * size, size) for m in range(D_PARTS)]
        opposite, side = [], []
        for m in range(D_PARTS):
            b_send[h, 0, spans[m]] = back(row_at(1, 2), m).astype(bf16)
            opposite.append(go(0, to_x, spans[m], m))
        for m in range(D_PARTS):
            side.append([])
            for n, s in enumerate(SIGNS):
                b_send[h, 1 + n, spans[m]] = back(row_at(1, s), m).astype(bf16)
                side[m].append(go(1 + n, to_y[s], spans[m], m))
        owners = (row_at(0, 2), row_at(0, 1), row_at(0, -1), row_at(1, 0), row)

        def compute(slot, m):
            def run():
                b_part[h, slot, spans[m]] = back(owners[slot], m)

            return later(run)

        computed = {(slot, m): compute(slot, m) for slot in range(5) for m in range(D_PARTS)}

        def reduce(m):
            last, after = [], []
            pieces = [pl.ds(m * size + n * (size // 2), size // 2) for n in range(2)]

            def across():
                yield [opposite[m], computed[0, m]]
                total = own(0, spans[m]) + came(0, spans[m])
                b_send[h, 3, spans[m]] = total.astype(bf16)
                work(0.1)
                turned = [go(3, to_y[-s], pieces[n], m) for n, s in enumerate(SIGNS)]
                for n, s in enumerate(SIGNS):
                    after.append(spawn(along(n, s, turned[1 - n])))

            def along(n, s, move):
                yield [move, computed[1 + n, m]]
                rows, rest = pieces[1 - n], pieces[n]
                total = own(1 + n, rows) + came(3, rows)
                b_send[h, 5 + n, rows] = total.astype(bf16)
                b_send[h, 5 + n, rest] = own(1 + n, rest).astype(bf16)
                work(0.1)
                last.append(go(5 + n, to_y[s], spans[m], m))

            def beside():
                yield side[m] + [computed[3, m]]
                total = own(3, spans[m]) + came(1, spans[m]) + came(2, spans[m])
                b_send[h, 4, spans[m]] = total.astype(bf16)
                work(0.1)
                last.append(go(4, to_x, spans[m], m))

            yield [spawn(across()), spawn(beside())]
            yield after
            yield last + [computed[4, m]]
            total = own(4, spans[m])
            for slot in (4, 5, 6):
                total = total + came(slot, spans[m])
            b_all[h, z, spans[m]] = total.astype(bf16)
            work(0.1)

        d_done[h] = [spawn(reduce(m)) for m in range(D_PARTS)]
        yield d_done[h] if D_PARTS == 1 else []

    def direction_part(owner, rows):
        work(0.4 if rows is ALL else 0.2)
        left = jnp.concatenate([b_all[h, owner, rows] for h in range(2)], axis=1)
        right = jnp.concatenate(
            [qr_all[h, owner].reshape(4 * COLS, HALF) for h in range(2)], axis=1
        )
        return lax.dot_general(
            left, right, (((1,), (1,)), ((), ())), preferred_element_type=f32
        )

    b_done, d_done = {}, {}
    seen, added = set(), []
    final = {}

    def add_direction(owner, what):
        def first():
            d_acc[...] = direction_part(owner, ALL)

        def add():
            d_acc[...] += direction_part(owner, ALL)

        if what in seen:
            if what == 0:
                added.append(later(first))
            else:
                added.append(later(add, added[0]))
        seen.add(what)

    def gather_z(h):
        count = {}

        def come(owner, what):
            count[what] = count.get(what, 0) + 1
            if count[what] == Z_PARTS:
                add_direction(owner, what)

        def along(n, m):
            if D_PARTS == 2:
                yield [d_done[h][m * 2 // Z_PARTS]]
            s = SIGNS[n]
            if n == 0:
                come(z, 0)
            view = b_all.at[h, z, ZPARTS[m]]
            move = same(view, to_z[s], "e", h, m, 0)
            for stage in (1, 2, 3):
                yield [move]
                owner = z_at(-s * stage)
                if stage < 3 or far_part(n, m):
                    view = b_all.at[h, owner, ZPARTS[m]]
                    move = same(view, to_z[s], "e", h, m, stage)
                come(owner, (n, stage))
            if far_part(n, m):
                final[h, m] = move

        yield [spawn(along(n, m)) for m in range(Z_PARTS) for n in range(2)]

    def pipeline(h):
        yield [right_tasks[h], grad_task]
        for part in (sum_z, gather_rotate, sum_row, gather_z):
            yield [spawn(part(h))]

    def finish(a):
        rows = PARTS[a]
        yield pipelines
        yield added
        yield [final[h, m] for h in range(2) for m in range(Z_PARTS) if m * 2 // Z_PARTS == a]
        d_acc[rows] += direction_part(z_at(4), rows)
        for m in range(2):
            d_send[m, rows] = d_acc[rows, block(2 * m + (1 - k))].astype(bf16)
        core = send(d_send.at[pl.ds(0, 2), rows], d_recv.at[pl.ds(0, 2), rows], to_core)
        yield [core]
        total = d_acc[rows, block(u_far)] + d_recv[1 - xh, rows].astype(f32)
        d_send[2, rows] = total.astype(bf16)
        far_copy = send(d_send.at[2, rows], d_recv.at[2, rows], to_far)
        yield [far_copy]
        total = d_acc[rows, block(u)] + d_recv[xh, rows].astype(f32)
        d_out[rows] = total + d_recv[2, rows].astype(f32)
        out_copies.append(move(d_out.at[rows], direction_out.at[rows]))

    out_copies = []
    left_task = spawn(gather_left())
    right_tasks = [spawn(gather_right(h)) for h in range(2)]
    grad_task = spawn(gather_grad())
    pipelines = [spawn(pipeline(h)) for h in range(2)]
    for a in range(2):
        spawn(finish(a))
    order.run()
    for copy in order.started:
        copy.wait_send()
    for copy in out_copies:
        copy.wait()


def on_device(weight, grad, moment_first, moment_second, basis_left, basis_right):
    block = (ROWS, COLS)
    half = (ROWS, HALF)
    anywhere = pl.BlockSpec(memory_space=pl.ANY)
    rotated, direction = pl.pallas_call(
        kernel,
        name="soap_step",
        out_shape=(jax.ShapeDtypeStruct(block, f32), jax.ShapeDtypeStruct(block, f32)),
        in_specs=[anywhere] * 5,
        out_specs=(anywhere,) * 2,
        scratch_shapes=[
            pltpu.VMEM(block, f32),
            pltpu.VMEM(block, f32),
            pltpu.VMEM((2, 8, 4, COLS, HALF), bf16),
            pltpu.VMEM((ROWS, 4 * COLS), bf16),
            pltpu.VMEM((8, 2, 2, 128, ROWS), bf16),
            pltpu.VMEM((2, 8) + half, bf16),
            pltpu.VMEM(block, f32),
            pltpu.VMEM(block, bf16),
            pltpu.VMEM((2, 2, 4) + half, f32),
            pltpu.VMEM((2, 2, 4) + half, bf16),
            pltpu.VMEM((2, 2, 4) + half, bf16),
            pltpu.VMEM((2, 5) + half, f32),
            pltpu.VMEM((2, 7) + half, bf16),
            pltpu.VMEM((2, 7) + half, bf16),
            pltpu.VMEM((2, 8) + half, bf16),
            pltpu.VMEM((ROWS, 4 * COLS), f32),
            pltpu.VMEM(block, f32),
            pltpu.VMEM((3,) + block, bf16),
            pltpu.VMEM((3,) + block, bf16),
            pltpu.SemaphoreType.DMA((N_MSG,)),
            pltpu.SemaphoreType.DMA((N_MSG,)),
            pltpu.SemaphoreType.DMA((16,)),
        ],
        compiler_params=pltpu.CompilerParams(
            collective_id=0, has_side_effects=True, vmem_limit_bytes=56 * 2**20
        ),
        cost_estimate=pl.CostEstimate(
            flops=6 * 2**30, bytes_accessed=4 * 2**20, transcendentals=0
        ),
    )(grad, moment_first, moment_second, basis_left, basis_right)
    first_new, second_new = new_moments(moment_first, moment_second, rotated)
    update = direction.astype(bf16)
    wide = weight.astype(f32)
    new_weight = (wide - learn_rate * (direction + decay_rate * wide)).astype(bf16)
    return new_weight, update, first_new, second_new


def solution(mesh):
    spec = P("row", "col")
    turned = P("col", "row")
    return jax.shard_map(
        on_device,
        mesh=mesh,
        in_specs=(spec, spec, spec, spec, turned, turned),
        out_specs=(spec,) * 4,
        check_vma=False,
    )
```
